32 devices in a mesh: segment: 16 (over z, x, core), fsdp: 2 (over y).
Axes of the slice: x: 2, y: 2, z: 4, core: 2. Of those that a mesh axis runs over, the one named last changes fastest.
Arguments:
- stream: bfloat16 [2, 16, 128, 4096], P(None, 'segment', 'fsdp'), may hold values from -60 to 60
- gain: bfloat16 [2, 16, 4096], P(None, 'segment'), may hold values from 0.099609375 to 1.8984375
- w_query: bfloat16 [2, 16, 32, 128, 128], P(None, 'segment', 'fsdp'), may hold values from -20 to 20
- w_key: bfloat16 [2, 16, 32, 128, 128], P(None, 'segment', 'fsdp'), may hold values from -20 to 20
- w_value: bfloat16 [2, 16, 32, 128, 128], P(None, 'segment', 'fsdp'), may hold values from -0.5 to 0.5
- w_mix: bfloat16 [2, 16, 128, 32, 32], P(None, 'segment', 'fsdp'), may hold values from -1 to 1
- active: int32 [2, 16], P(None, 'segment'), may hold values from 0 to 1
- random_blocks: int32 [2, 16, 2, 2], P(None, 'segment'), may hold values from 0 to 1
Outputs:
- advanced: bfloat16 [2, 16, 128, 4096], P(None, 'segment', 'fsdp')
The draws below stay inside these ranges and needn't reach their ends.
All inputs are finite; a program needn't handle non-finite values.
Results may differ from the reference program's by a relative error of at most 0.009.
Values may be sent and summed in bfloat16 or wider, within the bound.
A program may use at most 64 MiB of HBM per device.

```python
import math
import jax
import jax.numpy as jnp
from jax import lax

HEADS = 32
HS = 128
D = 4096
BLK = 64
R = 2
V = 2
ROUNDS = 2
SEQ = 128
NB = 2
N_SEGMENT = 16


def draw_stream(key, part):
    own_key = jax.random.fold_in(key, 101)
    first, second, third = jax.random.split(own_key, 3)
    shape = (V, N_SEGMENT, SEQ, D)
    row_scale = jnp.exp(jax.random.uniform(second, (V, N_SEGMENT, SEQ, 1), jnp.float32, math.log(0.3), math.log(3.0)))
    col_scale = jnp.exp(jax.random.uniform(third, (V, N_SEGMENT, 1, D), jnp.float32, math.log(0.3), math.log(3.0)))
    base = jnp.clip(jax.random.normal(first, shape, jnp.float32), -6.0, 6.0)
    return (base * row_scale * col_scale).astype(jnp.bfloat16)


def draw_w_query(key, part):
    own_key = jax.random.fold_in(key, 202)
    shape = (V, N_SEGMENT, HEADS, HS, HS)
    base = jnp.clip(jax.random.normal(own_key, shape, jnp.float32), -6.0, 6.0) * HS ** (-0.5)
    return base.astype(jnp.bfloat16)


def draw_w_key(key, part):
    own_key = jax.random.fold_in(key, 303)
    shape = (V, N_SEGMENT, HEADS, HS, HS)
    base = jnp.clip(jax.random.normal(own_key, shape, jnp.float32), -6.0, 6.0) * HS ** (-0.5)
    return base.astype(jnp.bfloat16)


def plant(drawn, key, low, top_value):
    shape = drawn.shape
    spot = [jax.random.randint(jax.random.fold_in(key, axis), (), 0, shape[axis]) for axis in range(len(shape))]
    drawn = drawn.at[tuple(spot)].set(low)
    longest = shape.index(max(shape))
    spot[longest] = (spot[longest] + 1) % shape[longest]
    return drawn.at[tuple(spot)].set(top_value)


def shard_levels(key, extent, pieces, least, high):
    level = 1.0
    for dim, blocks in pieces:
        draws = jax.random.uniform(jax.random.fold_in(jax.random.fold_in(key, 6), dim), (blocks,), jnp.float32, least / len(pieces), high / len(pieces))
        level = level * jnp.repeat(jnp.exp(draws), extent[dim] // blocks).reshape((-1,) + (1,) * (len(extent) - 1 - dim))
    return level


def bell_draw(key, shape, deviation, limit, cuts=(), held_as=jnp.bfloat16):
    level = shard_levels(key, shape, cuts, -0.22, 0.18) if cuts else 1.0
    drawn = jax.random.normal(key, shape, jnp.float32) * deviation * level
    return jnp.minimum(jnp.maximum(drawn, -limit), limit).astype(held_as)


def setup_inputs(seed: int = 0) -> dict:
    streams_of = jax.random.split(jax.random.key(seed), 9)
    stream = draw_stream(jax.random.fold_in(streams_of[8], 71), 0)
    gain = jnp.clip(1.0 + 0.18 * jax.random.normal(streams_of[1], (V, N_SEGMENT, D), jnp.float32), 0.099609375, 1.8984375).astype(jnp.bfloat16)
    w_query = draw_w_query(jax.random.fold_in(streams_of[8], 71), 0)
    w_key = draw_w_key(jax.random.fold_in(streams_of[8], 71), 0)
    w_value = bell_draw(streams_of[4], (V, N_SEGMENT, HEADS, HS, HS), HS ** -0.5, 0.5, ((1, 16), (2, 2)))
    w_mix = bell_draw(streams_of[5], (V, N_SEGMENT, HS, HEADS, HEADS), HEADS ** -0.5, 1.0, ((1, 16), (2, 2)))
    active = plant(jax.random.randint(streams_of[6], (V, N_SEGMENT), 0, 2), jax.random.fold_in(streams_of[6], 1), 0, 1).astype(jnp.int32)
    random_blocks = plant(jax.random.randint(streams_of[7], (V, N_SEGMENT, NB, R), 0, NB), jax.random.fold_in(streams_of[7], 1), 0, NB - 1).astype(jnp.int32)
    return {"stream": stream, "gain": gain, "w_query": w_query, "w_key": w_key, "w_value": w_value, "w_mix": w_mix, "active": active, "random_blocks": random_blocks}


EPS = 1e-05

def block_attention(query, keys, values, random_ids):
    count = SEQ // BLK
    query_blocks = query.reshape(count, BLK, HEADS, HS).astype(jnp.float32)
    key_blocks = keys.reshape(count, BLK, HEADS, HS)
    value_blocks = values.reshape(count, BLK, HEADS, HS)
    block_ids = jnp.arange(count, dtype=jnp.int32)
    window = jnp.stack([(block_ids - 1) % count, block_ids, (block_ids + 1) % count, jnp.zeros_like(block_ids)], axis=1)
    chosen = jnp.concatenate([window, random_ids.astype(jnp.int32)], axis=1)
    picked_keys = key_blocks[chosen].reshape(count, chosen.shape[1] * BLK, HEADS, HS).astype(jnp.float32)
    picked_values = value_blocks[chosen].reshape(count, chosen.shape[1] * BLK, HEADS, HS).astype(jnp.float32)
    scores = jnp.einsum('nqhd,nkhd->nhqk', query_blocks, picked_keys)
    row_max = lax.optimization_barrier(jnp.max(scores, axis=-1, keepdims=True))
    powers = jnp.exp(scores - row_max)
    weights = (powers / lax.optimization_barrier(jnp.sum(powers, axis=-1, keepdims=True))).astype(jnp.bfloat16)
    mixed = jnp.einsum('nhqk,nkhd->nqhd', weights.astype(jnp.float32), picked_values).astype(jnp.bfloat16)
    return mixed.reshape(SEQ, HEADS, HS)

def layer(state, gains, queries_w, keys_w, values_w, mix_w, live, random_ids):
    wide = state.astype(jnp.float32)
    mean_sq = lax.optimization_barrier(jnp.mean(wide * wide, axis=1, keepdims=True))
    normed = (wide * lax.rsqrt(mean_sq + EPS) * gains.astype(jnp.float32)).astype(jnp.bfloat16)
    view = normed.reshape(SEQ, HEADS, HS).astype(jnp.float32)
    raw = jnp.einsum('thc,hcd->thd', view, queries_w.astype(jnp.float32))
    query = (raw * HS ** (-0.5)).astype(jnp.bfloat16)
    keys = jnp.einsum('thc,hcd->thd', view, keys_w.astype(jnp.float32)).astype(jnp.bfloat16)
    values = jnp.einsum('thc,hcd->thd', view, values_w.astype(jnp.float32)).astype(jnp.bfloat16)
    attended = block_attention(query, keys, values, random_ids)
    mixed = jnp.einsum('thc,chg->tgc', attended.astype(jnp.float32), mix_w.astype(jnp.float32)).astype(jnp.bfloat16)
    updated = (wide + mixed.reshape(SEQ, D).astype(jnp.float32)).astype(jnp.bfloat16)
    return jnp.where(live > 0, updated, state)

def reference(stream, gain, w_query, w_key, w_value, w_mix, active, random_blocks):
    count = V * N_SEGMENT
    flat = stream.reshape(count, SEQ, D)
    params = (gain.reshape(count, D), w_query.reshape(count, HEADS, HS, HS), w_key.reshape(count, HEADS, HS, HS), w_value.reshape(count, HEADS, HS, HS), w_mix.reshape(count, HS, HEADS, HEADS), active.reshape(count), random_blocks.reshape(count, NB, R))

    def apply_layer(items):
        extra = items[1]
        return layer(items[0], extra[0], extra[1], extra[2], extra[3], extra[4], extra[5], extra[6])
    for round_index in range(ROUNDS):
        flat = jnp.roll(lax.map(apply_layer, (flat, params)), 1, axis=0)
    return flat.reshape(V, N_SEGMENT, SEQ, D)
```

```python
import functools

import jax
import jax.numpy as jnp
from jax import lax
from jax.experimental import pallas as pl
from jax.experimental.pallas import tpu as pltpu
from jax.sharding import PartitionSpec as P

BLK = 64
ROUNDS = 2
EPS = 1e-05
LANES = 128
MESH = pl.DeviceIdType.MESH
F32 = jnp.float32
BF16 = jnp.bfloat16


def kernel(
    segments, peers, stream, gain, wq, wk, wv, wm, live, ids, out,
    st_in, xn, gath, att_out, att_in, st_out, wm_all, wm_t, counts,
    x_send, x_recv, a_send, a_recv, s_send, s_recv, m_send, m_recv,
):
    virtual, tokens, width = stream.shape
    local_heads, hs = wq.shape[1], wq.shape[2]
    heads = width // hs
    seq = tokens * peers
    blocks = seq // BLK
    randoms = ids.shape[2]
    s = lax.axis_index("segment")
    f = lax.axis_index("fsdp")
    ahead = lax.rem(s + 1, segments)
    behind = lax.rem(s + segments - 1, segments)

    barrier = pltpu.get_barrier_semaphore()
    for d in range(1, peers):
        pl.semaphore_signal(barrier, inc=1, device_id=(s, lax.rem(f + d, peers)), device_id_type=MESH)
    for other in (ahead, behind):
        pl.semaphore_signal(barrier, inc=1, device_id=(other, f), device_id_type=MESH)
    pl.semaphore_wait(barrier, peers + 1)

    def to_peer(d):
        return lax.rem(f + d, peers)

    def from_peer(d):
        return lax.rem(f + peers - d, peers)

    def x_copy(r, v, d, landing=False):
        slot = from_peer(d) if landing else f
        return pltpu.make_async_remote_copy(
            src_ref=xn.at[r, v, to_peer(d)], dst_ref=gath.at[r, v, slot],
            send_sem=x_send.at[r, v, d - 1], recv_sem=x_recv.at[r, v, d - 1],
            device_id=(s, to_peer(d)), device_id_type=MESH)

    def a_copy(r, v, d, landing=False):
        slot = from_peer(d) if landing else f
        return pltpu.make_async_remote_copy(
            src_ref=att_out.at[r, v, to_peer(d)], dst_ref=att_in.at[r, v, slot],
            send_sem=a_send.at[r, v, d - 1], recv_sem=a_recv.at[r, v, d - 1],
            device_id=(s, to_peer(d)), device_id_type=MESH)

    def m_copy(d, landing=False):
        slot = from_peer(d) if landing else f
        return pltpu.make_async_remote_copy(
            src_ref=wm, dst_ref=wm_all.at[slot],
            send_sem=m_send.at[d - 1], recv_sem=m_recv.at[d - 1],
            device_id=(s, to_peer(d)), device_id_type=MESH)

    def s_copy(r, v, landing=False):
        at = v if landing else lax.rem(v + jnp.where(s == segments - 1, 1, 0), virtual)
        target = out if r == ROUNDS - 1 else st_in.at[r]
        return pltpu.make_async_remote_copy(
            src_ref=st_out.at[r, v], dst_ref=target.at[at],
            send_sem=s_send.at[r, v], recv_sem=s_recv.at[r, at],
            device_id=(ahead, f), device_id_type=MESH)

    def state_of(r):
        return stream if r == 0 else st_in.at[r - 1]

    def order(r):
        return [lax.rem(o + jnp.where(s < r, 1, 0), virtual) for o in range(virtual)]

    def norm(r, v):
        state = state_of(r)

        def rows_body(i, carry):
            rows = pl.ds(pl.multiple_of(i * 16, 16), 16)
            total = jnp.zeros((16, LANES), F32)
            for c in range(width // LANES):
                wide = state[v, rows, c * LANES:(c + 1) * LANES].astype(F32)
                total = total + wide * wide
            scale = lax.rsqrt(jnp.sum(total, axis=1, keepdims=True) / width + EPS)
            for c in range(heads):
                wide = state[v, rows, c * hs:(c + 1) * hs].astype(F32)
                g = gain[v, :, c * hs:(c + 1) * hs].astype(F32)
                j, at = c // local_heads, (c % local_heads) * hs
                xn[r, v, j, rows, at:at + hs] = (wide * scale * g).astype(BF16)
            return carry

        lax.fori_loop(0, tokens // 16, rows_body, 0)

    def count_blocks():
        lane_block = lax.broadcasted_iota(jnp.int32, (BLK, seq), 1) // BLK
        for v in range(virtual):
            for i in range(blocks):
                window = [(i - 1) % blocks, i, (i + 1) % blocks, 0]
                total = jnp.zeros((BLK, seq), F32)
                for b in window:
                    total = total + jnp.where(lane_block == b, 1.0, 0.0)
                for k in range(randoms):
                    total = total + jnp.where(lane_block == ids[v, i, k], 1.0, 0.0)
                counts[v, i * BLK:(i + 1) * BLK, :] = total

    def attention(r, v):
        step = 4 if local_heads % 4 == 0 else 1

        def one_head(h):
            lanes = pl.ds(pl.multiple_of(h * hs, hs), hs)
            x = gath[r, v, :, :, lanes].reshape(seq, hs)
            q = (jnp.dot(x, wq[v, h], preferred_element_type=F32) * hs ** (-0.5)).astype(BF16)
            k = jnp.dot(x, wk[v, h], preferred_element_type=F32).astype(BF16)
            val = jnp.dot(x, wv[v, h], preferred_element_type=F32).astype(BF16)
            scores = lax.dot_general(q, k, (((1,), (1,)), ((), ())), preferred_element_type=F32)
            count = counts[v]
            scores = jnp.where(count > 0.0, scores, -3e38)
            powers = jnp.exp(scores - jnp.max(scores, axis=1, keepdims=True)) * count
            weights = (powers * (1.0 / jnp.sum(powers, axis=1, keepdims=True))).astype(BF16)
            att = jnp.dot(weights, val, preferred_element_type=F32).astype(BF16)
            att_out[r, v, :, :, lanes] = att.reshape(peers, tokens, hs)

        def body(i, carry):
            for u in range(step):
                one_head(i * step + u)
            return carry

        lax.fori_loop(0, local_heads // step, body, 0)

    def turn_mix():
        wm_all[f] = wm[...]
        for v in range(virtual):
            def body(i, carry):
                at = pl.ds(pl.multiple_of(i * LANES, LANES), LANES)
                part = wm_all[:, v, :, at].reshape(hs, LANES).astype(F32)
                wm_t[v, at, :] = part.T
                return carry
            lax.fori_loop(0, heads * heads // LANES, body, 0)

    def mix(r, v):
        state = state_of(r)
        half = 32
        on = jnp.full((half, hs), live[v].astype(F32))

        def body(i, carry):
            group = i // (tokens // half)
            rows = pl.ds(pl.multiple_of(lax.rem(i, tokens // half) * half, half), half)
            sums = [jnp.zeros((half, hs), F32) for _ in range(8)]
            for h in range(heads):
                j, at = h // local_heads, (h % local_heads) * hs
                a = att_in[r, v, j, rows, at:at + hs].astype(F32)
                w = wm_t[v, pl.ds(pl.multiple_of(h * heads + group * 8, 8), 8), :]
                for g in range(8):
                    sums[g] = sums[g] + a * w[g:g + 1]
            for g in range(8):
                lanes = pl.ds(pl.multiple_of((group * 8 + g) * hs, hs), hs)
                wide = state[v, rows, lanes].astype(F32)
                updated = wide + sums[g].astype(BF16).astype(F32)
                st_out[r, v, rows, lanes] = jnp.where(on > 0.0, updated, wide).astype(BF16)
            return carry

        lax.fori_loop(0, (heads // 8) * (tokens // half), body, 0)

    for r in range(ROUNDS):
        todo = order(r)
        for v in todo:
            if r > 0:
                s_copy(r - 1, v, landing=True).wait_recv()
            norm(r, v)
            for d in range(1, peers):
                x_copy(r, v, d).start()
            gath[r, v, f] = xn[r, v, f]
        if r == 0:
            for d in range(1, peers):
                m_copy(d).start()
            count_blocks()
        for v in todo:
            for d in range(1, peers):
                x_copy(r, v, d, landing=True).wait_recv()
            attention(r, v)
            for d in range(1, peers):
                a_copy(r, v, d).start()
            att_in[r, v, f] = att_out[r, v, f]
        if r == 0:
            for d in range(1, peers):
                m_copy(d, landing=True).wait_recv()
            turn_mix()
        for v in todo:
            for d in range(1, peers):
                a_copy(r, v, d, landing=True).wait_recv()
            mix(r, v)
            s_copy(r, v).start()

    for v in range(virtual):
        s_copy(ROUNDS - 1, v, landing=True).wait_recv()
    for r in range(ROUNDS):
        for v in range(virtual):
            for d in range(1, peers):
                x_copy(r, v, d).wait_send()
                a_copy(r, v, d).wait_send()
            s_copy(r, v).wait_send()
    for d in range(1, peers):
        m_copy(d).wait_send()


def shards(segments, peers, stream, gain, w_query, w_key, w_value, w_mix, active, random_blocks):
    virtual, _, tokens, width = stream.shape
    local_heads, hs = w_query.shape[2], w_query.shape[3]
    heads = width // hs
    local = w_mix.shape[2]
    seq = tokens * peers
    group = local_heads * hs
    vmem = pl.BlockSpec(memory_space=pltpu.VMEM)
    smem = pl.BlockSpec(memory_space=pltpu.SMEM)
    dma = pltpu.SemaphoreType.DMA
    apart = max(peers - 1, 1)
    result = pl.pallas_call(
        functools.partial(kernel, segments, peers),
        out_shape=jax.ShapeDtypeStruct((virtual, tokens, width), BF16),
        in_specs=[vmem] * 6 + [smem] * 2,
        out_specs=pl.BlockSpec(memory_space=pl.ANY),
        scratch_shapes=[
            pltpu.VMEM((max(ROUNDS - 1, 1), virtual, tokens, width), BF16),
            pltpu.VMEM((ROUNDS, virtual, peers, tokens, group), BF16),
            pltpu.VMEM((ROUNDS, virtual, peers, tokens, group), BF16),
            pltpu.VMEM((ROUNDS, virtual, peers, tokens, group), BF16),
            pltpu.VMEM((ROUNDS, virtual, peers, tokens, group), BF16),
            pltpu.VMEM((ROUNDS, virtual, tokens, width), BF16),
            pltpu.VMEM((peers, virtual, local, heads * heads), BF16),
            pltpu.VMEM((virtual, heads * heads, hs), F32),
            pltpu.VMEM((virtual, seq, seq), F32),
            dma((ROUNDS, virtual, apart)),
            dma((ROUNDS, virtual, apart)),
            dma((ROUNDS, virtual, apart)),
            dma((ROUNDS, virtual, apart)),
            dma((ROUNDS, virtual)),
            dma((ROUNDS, virtual)),
            dma((apart,)),
            dma((apart,)),
        ],
        compiler_params=pltpu.CompilerParams(
            collective_id=0, has_side_effects=True, vmem_limit_bytes=56 * 1024 * 1024
        ),
        cost_estimate=pl.CostEstimate(
            flops=ROUNDS * virtual * seq * local_heads * hs * (6 * hs + 4 * seq),
            bytes_accessed=6 * 1024 * 1024,
            transcendentals=ROUNDS * virtual * seq * local_heads * seq,
        ),
    )(
        stream[:, 0],
        gain.reshape(virtual, 1, width),
        w_query[:, 0],
        w_key[:, 0],
        w_value[:, 0],
        w_mix.reshape(virtual, local, heads * heads),
        active[:, 0],
        random_blocks[:, 0],
    )
    return result[:, None]


def solution(mesh):
    in_specs = (
        P(None, "segment", "fsdp", None),
        P(None, "segment", None),
        P(None, "segment", "fsdp", None, None),
        P(None, "segment", "fsdp", None, None),
        P(None, "segment", "fsdp", None, None),
        P(None, "segment", "fsdp", None, None),
        P(None, "segment"),
        P(None, "segment", None, None),
    )
    out_specs = P(None, "segment", "fsdp", None)
    body = functools.partial(shards, mesh.shape["segment"], mesh.shape["fsdp"])
    return jax.shard_map(body, mesh=mesh, in_specs=in_specs, out_specs=out_specs, check_vma=False)
```

```python
import functools

import jax
import jax.numpy as jnp
from jax import lax
from jax.experimental import pallas as pl
from jax.experimental.pallas import tpu as pltpu
from jax.sharding import PartitionSpec as P

BLK = 64
ROUNDS = 2
EPS = 1e-05
LANES = 128
PIECES = 2
MESH = pl.DeviceIdType.MESH
F32 = jnp.float32
BF16 = jnp.bfloat16


def kernel(
    segments, peers, stream_hbm, gain_in, wq_hbm, wk_hbm, wv_hbm, wm, live, ids, out,
    stream, gain, wq, wk, wv,
    st_in, xn, gath, att_out, att_in, st_out, wm_all, wm_t, counts,
    x_send, x_recv, a_send, a_recv, s_send, s_recv, m_send, m_recv, load_sem,
):
    virtual, tokens, width = stream.shape
    local_heads, hs = wq.shape[1], wq.shape[2]
    half = tokens // PIECES
    part = local_heads // PIECES
    local = wm.shape[2]
    heads = width // hs
    seq = tokens * peers
    blocks = seq // BLK
    randoms = ids.shape[2]
    s = lax.axis_index("segment")
    f = lax.axis_index("fsdp")
    ahead = lax.rem(s + 1, segments)
    behind = lax.rem(s + segments - 1, segments)

    barrier = pltpu.get_barrier_semaphore()
    for d in range(1, peers):
        pl.semaphore_signal(barrier, inc=1, device_id=(s, lax.rem(f + d, peers)), device_id_type=MESH)
    for other in (ahead, behind):
        pl.semaphore_signal(barrier, inc=1, device_id=(other, f), device_id_type=MESH)

    def load(n, v):
        source, target = ((stream_hbm, stream), (wq_hbm, wq), (wk_hbm, wk), (wv_hbm, wv))[n]
        return pltpu.make_async_copy(source.at[v], target.at[v], load_sem.at[n, v])

    for n in range(4):
        for v in range(virtual):
            load(n, v).start()

    def to_peer(d):
        return lax.rem(f + d, peers)

    def from_peer(d):
        return lax.rem(f + peers - d, peers)

    def x_copy(r, v, d, pc, hh, landing=False):
        slot = from_peer(d) if landing else f
        rows, lanes = pl.ds(pc * half, half), pl.ds(hh * part * hs, part * hs)
        return pltpu.make_async_remote_copy(
            src_ref=xn.at[r, v, to_peer(d), rows, lanes], dst_ref=gath.at[r, v, slot, rows, lanes],
            send_sem=x_send.at[r, v, d - 1, pc, hh], recv_sem=x_recv.at[r, v, d - 1, pc, hh],
            device_id=(s, to_peer(d)), device_id_type=MESH)

    def a_copy(r, v, d, pc, hh, landing=False):
        slot = from_peer(d) if landing else f
        rows, lanes = pl.ds(pc * half, half), pl.ds(hh * part * hs, part * hs)
        return pltpu.make_async_remote_copy(
            src_ref=att_out.at[r, v, to_peer(d), rows, lanes], dst_ref=att_in.at[r, v, slot, rows, lanes],
            send_sem=a_send.at[r, v, d - 1, pc, hh], recv_sem=a_recv.at[r, v, d - 1, pc, hh],
            device_id=(s, to_peer(d)), device_id_type=MESH)

    def m_copy(d, landing=False):
        slot = from_peer(d) if landing else f
        return pltpu.make_async_remote_copy(
            src_ref=wm_all.at[f], dst_ref=wm_all.at[slot],
            send_sem=m_send.at[d - 1], recv_sem=m_recv.at[d - 1],
            device_id=(s, to_peer(d)), device_id_type=MESH)

    def s_copy(r, v, pc, landing=False):
        at = v if landing else lax.rem(v + jnp.where(s == segments - 1, 1, 0), virtual)
        target = out if r == ROUNDS - 1 else st_in.at[r]
        rows = pl.ds(pc * half, half)
        return pltpu.make_async_remote_copy(
            src_ref=st_out.at[r, v, rows], dst_ref=target.at[at, rows],
            send_sem=s_send.at[r, v, pc], recv_sem=s_recv.at[r, at, pc],
            device_id=(ahead, f), device_id_type=MESH)

    def state_of(r):
        return stream if r == 0 else st_in.at[r - 1]

    def order(r):
        if r == 0:
            return list(range(virtual))
        return [lax.rem(o + jnp.where(s < r, 1, 0), virtual) for o in range(virtual)]

    def norm(r, v, pc):
        state = state_of(r)

        def rows_body(i, carry):
            rows = pl.ds(pl.multiple_of(pc * half + i * 16, 16), 16)
            total = jnp.zeros((16, LANES), F32)
            for c in range(width // LANES):
                wide = state[v, rows, c * LANES:(c + 1) * LANES].astype(F32)
                total = total + wide * wide
            scale = lax.rsqrt(jnp.sum(total, axis=1, keepdims=True) / width + EPS)
            for c in range(heads):
                wide = state[v, rows, c * hs:(c + 1) * hs].astype(F32)
                g = gain[v, :, c * hs:(c + 1) * hs]
                j, at = c // local_heads, (c % local_heads) * hs
                xn[r, v, j, rows, at:at + hs] = (wide * scale * g).astype(BF16)
            return carry

        lax.fori_loop(0, half // 16, rows_body, 0)

    def count_blocks():
        lane_block = lax.broadcasted_iota(jnp.int32, (BLK, seq), 1) // BLK
        for v in range(virtual):
            for i in range(blocks):
                window = [(i - 1) % blocks, i, (i + 1) % blocks, 0]
                total = jnp.zeros((BLK, seq), F32)
                for b in window:
                    total = total + jnp.where(lane_block == b, 1.0, 0.0)
                for k in range(randoms):
                    total = total + jnp.where(lane_block == ids[v, i, k], 1.0, 0.0)
                counts[v, i * BLK:(i + 1) * BLK, :] = total

    def attention(r, v, hh):
        step = 4 if part % 4 == 0 else 1

        def one_head(h):
            lanes = pl.ds(pl.multiple_of(h * hs, hs), hs)
            x = gath[r, v, :, :, lanes].reshape(seq, hs)
            q = (jnp.dot(x, wq[v, h], preferred_element_type=F32) * hs ** (-0.5)).astype(BF16)
            k = jnp.dot(x, wk[v, h], preferred_element_type=F32).astype(BF16)
            val = jnp.dot(x, wv[v, h], preferred_element_type=F32).astype(BF16)
            scores = lax.dot_general(q, k, (((1,), (1,)), ((), ())), preferred_element_type=F32)
            count = counts[v]
            scores = jnp.where(count > 0.0, scores, -3e38)
            powers = jnp.exp(scores - jnp.max(scores, axis=1, keepdims=True)) * count
            weights = (powers * (1.0 / jnp.sum(powers, axis=1, keepdims=True))).astype(BF16)
            att = jnp.dot(weights, val, preferred_element_type=F32).astype(BF16)
            att_out[r, v, :, :, lanes] = att.reshape(peers, tokens, hs)

        def body(i, carry):
            for u in range(step):
                one_head(hh * part + i * step + u)
            return carry

        lax.fori_loop(0, part // step, body, 0)

    def pack_mix():
        def body(i, carry):
            rows = pl.ds(pl.multiple_of(i * LANES, LANES), LANES)
            both = [wm[v, rows, :].astype(F32) for v in range(virtual)]
            wm_all[f, rows, :] = jnp.concatenate(both, axis=1).astype(BF16)
            return carry

        lax.fori_loop(0, heads * heads // LANES, body, 0)

    def spread_mix():
        def body(i, carry):
            rows = pl.ds(pl.multiple_of(i * LANES, LANES), LANES)
            each = [wm_all[j, rows, :].astype(F32) for j in range(peers)]
            for v in range(virtual):
                wm_t[v, rows, :] = jnp.concatenate(
                    [e[:, v * local:(v + 1) * local] for e in each], axis=1)
            return carry

        lax.fori_loop(0, heads * heads // LANES, body, 0)

    def mix(r, v, pc):
        state = state_of(r)
        on = jnp.full((half, hs), live[v].astype(F32))

        rows = pl.ds(pc * half, half)

        def body(group, carry):
            sums = [jnp.zeros((half, hs), F32) for _ in range(8)]
            for h in range(heads):
                j, at = h // local_heads, (h % local_heads) * hs
                a = att_in[r, v, j, rows, at:at + hs].astype(F32)
                w = wm_t[v, pl.ds(pl.multiple_of(h * heads + group * 8, 8), 8), :]
                for g in range(8):
                    sums[g] = sums[g] + a * w[g:g + 1]
            for g in range(8):
                lanes = pl.ds(pl.multiple_of((group * 8 + g) * hs, hs), hs)
                wide = state[v, rows, lanes].astype(F32)
                updated = wide + sums[g].astype(BF16).astype(F32)
                st_out[r, v, rows, lanes] = jnp.where(on > 0.0, updated, wide).astype(BF16)
            return carry

        lax.fori_loop(0, heads // 8, body, 0)

    others = range(1, peers)
    pieces = range(PIECES)
    for r in range(ROUNDS):
        todo = order(r)
        for o, v in enumerate(todo):
            if r == 0:
                load(0, v).wait()
                gain[v] = gain_in[v:v + 1, :].astype(F32)
            for pc in pieces:
                if r > 0:
                    s_copy(r - 1, v, pc, landing=True).wait_recv()
                norm(r, v, pc)
                if r == 0 and o == 0 and pc == 0:
                    pl.semaphore_wait(barrier, peers + 1)
                for hh in pieces:
                    for d in others:
                        x_copy(r, v, d, pc, hh).start()
            gath[r, v, f] = xn[r, v, f]
        if r == 0:
            pack_mix()
            for d in others:
                m_copy(d).start()
            count_blocks()
        for v in todo:
            if r == 0:
                for n in range(1, 4):
                    load(n, v).wait()
            for hh in pieces:
                for d in others:
                    for pc in pieces:
                        x_copy(r, v, d, pc, hh, landing=True).wait_recv()
                attention(r, v, hh)
                for pc in pieces:
                    for d in others:
                        a_copy(r, v, d, pc, hh).start()
            att_in[r, v, f] = att_out[r, v, f]
        if r == 0:
            for d in others:
                m_copy(d, landing=True).wait_recv()
            spread_mix()
        for v in todo:
            for pc in pieces:
                for d in others:
                    for hh in pieces:
                        a_copy(r, v, d, pc, hh, landing=True).wait_recv()
                mix(r, v, pc)
                s_copy(r, v, pc).start()

    for v in range(virtual):
        for pc in pieces:
            s_copy(ROUNDS - 1, v, pc, landing=True).wait_recv()
    for r in range(ROUNDS):
        for v in range(virtual):
            for pc in pieces:
                for d in others:
                    for hh in pieces:
                        x_copy(r, v, d, pc, hh).wait_send()
                        a_copy(r, v, d, pc, hh).wait_send()
                s_copy(r, v, pc).wait_send()
    for d in others:
        m_copy(d).wait_send()


def shards(segments, peers, stream, gain, w_query, w_key, w_value, w_mix, active, random_blocks):
    virtual, _, tokens, width = stream.shape
    local_heads, hs = w_query.shape[2], w_query.shape[3]
    heads = width // hs
    local = w_mix.shape[2]
    seq = tokens * peers
    group = local_heads * hs
    vmem = pl.BlockSpec(memory_space=pltpu.VMEM)
    hbm = pl.BlockSpec(memory_space=pl.ANY)
    smem = pl.BlockSpec(memory_space=pltpu.SMEM)
    dma = pltpu.SemaphoreType.DMA
    apart = max(peers - 1, 1)
    result = pl.pallas_call(
        functools.partial(kernel, segments, peers),
        out_shape=jax.ShapeDtypeStruct((virtual, tokens, width), BF16),
        in_specs=[hbm, vmem, hbm, hbm, hbm, vmem, smem, smem],
        out_specs=pl.BlockSpec(memory_space=pl.ANY),
        scratch_shapes=[
            pltpu.VMEM((virtual, tokens, width), BF16),
            pltpu.VMEM((virtual, 1, width), F32),
            pltpu.VMEM((virtual, local_heads, hs, hs), BF16),
            pltpu.VMEM((virtual, local_heads, hs, hs), BF16),
            pltpu.VMEM((virtual, local_heads, hs, hs), BF16),
            pltpu.VMEM((max(ROUNDS - 1, 1), virtual, tokens, width), BF16),
            pltpu.VMEM((ROUNDS, virtual, peers, tokens, group), BF16),
            pltpu.VMEM((ROUNDS, virtual, peers, tokens, group), BF16),
            pltpu.VMEM((ROUNDS, virtual, peers, tokens, group), BF16),
            pltpu.VMEM((ROUNDS, virtual, peers, tokens, group), BF16),
            pltpu.VMEM((ROUNDS, virtual, tokens, width), BF16),
            pltpu.VMEM((peers, heads * heads, virtual * local), BF16),
            pltpu.VMEM((virtual, heads * heads, hs), F32),
            pltpu.VMEM((virtual, seq, seq), F32),
            dma((ROUNDS, virtual, apart, PIECES, PIECES)),
            dma((ROUNDS, virtual, apart, PIECES, PIECES)),
            dma((ROUNDS, virtual, apart, PIECES, PIECES)),
            dma((ROUNDS, virtual, apart, PIECES, PIECES)),
            dma((ROUNDS, virtual, PIECES)),
            dma((ROUNDS, virtual, PIECES)),
            dma((apart,)),
            dma((apart,)),
            dma((4, virtual)),
        ],
        compiler_params=pltpu.CompilerParams(
            collective_id=0, has_side_effects=True, vmem_limit_bytes=56 * 1024 * 1024
        ),
        cost_estimate=pl.CostEstimate(
            flops=ROUNDS * virtual * seq * local_heads * hs * (6 * hs + 4 * seq),
            bytes_accessed=6 * 1024 * 1024,
            transcendentals=ROUNDS * virtual * seq * local_heads * seq,
        ),
    )(
        stream[:, 0],
        gain[:, 0],
        w_query[:, 0],
        w_key[:, 0],
        w_value[:, 0],
        w_mix[:, 0].transpose(0, 2, 3, 1).reshape(virtual, heads * heads, local),
        active[:, 0],
        random_blocks[:, 0],
    )
    return result[:, None]


def solution(mesh):
    in_specs = (
        P(None, "segment", "fsdp", None),
        P(None, "segment", None),
        P(None, "segment", "fsdp", None, None),
        P(None, "segment", "fsdp", None, None),
        P(None, "segment", "fsdp", None, None),
        P(None, "segment", "fsdp", None, None),
        P(None, "segment"),
        P(None, "segment", None, None),
    )
    out_specs = P(None, "segment", "fsdp", None)
    body = functools.partial(shards, mesh.shape["segment"], mesh.shape["fsdp"])
    return jax.shard_map(body, mesh=mesh, in_specs=in_specs, out_specs=out_specs, check_vma=False)
```

```python
import functools

import jax
import jax.numpy as jnp
from jax import lax
from jax.experimental import pallas as pl
from jax.experimental.pallas import tpu as pltpu
from jax.sharding import PartitionSpec as P

BLK = 64
ROUNDS = 2
EPS = 1e-05
LANES = 128
PIECES = 2
MESH = pl.DeviceIdType.MESH
F32 = jnp.float32
BF16 = jnp.bfloat16


def kernel(
    segments, peers, stream_hbm, gain_in, wq_hbm, wk_hbm, wv_hbm, wm, live, ids, out,
    stream, gain, wq, wk, wv,
    st_in, xn, gath, att_out, att_in, st_out, wm_all, wm_t, counts,
    x_send, x_recv, a_send, a_recv, s_send, s_recv, m_send, m_recv, load_sem,
):
    virtual, tokens, width = stream.shape
    local_heads, hs = wq.shape[1], wq.shape[2]
    half = tokens // PIECES
    part = local_heads // PIECES
    local = wm.shape[2]
    heads = width // hs
    seq = tokens * peers
    blocks = seq // BLK
    randoms = ids.shape[2]
    s = lax.axis_index("segment")
    f = lax.axis_index("fsdp")
    ahead = lax.rem(s + 1, segments)
    behind = lax.rem(s + segments - 1, segments)

    barrier = pltpu.get_barrier_semaphore()
    for d in range(1, peers):
        pl.semaphore_signal(barrier, inc=1, device_id=(s, lax.rem(f + d, peers)), device_id_type=MESH)
    for other in (ahead, behind):
        pl.semaphore_signal(barrier, inc=1, device_id=(other, f), device_id_type=MESH)

    def load(n, v):
        source, target = ((stream_hbm, stream), (wq_hbm, wq), (wk_hbm, wk), (wv_hbm, wv))[n]
        return pltpu.make_async_copy(source.at[v], target.at[v], load_sem.at[n, v])

    for n in range(4):
        for v in range(virtual):
            load(n, v).start()

    def to_peer(d):
        return lax.rem(f + d, peers)

    def from_peer(d):
        return lax.rem(f + peers - d, peers)

    def x_copy(r, v, d, pc, hh, landing=False):
        slot = from_peer(d) if landing else f
        rows, lanes = pl.ds(pc * half, half), pl.ds(hh * part * hs, part * hs)
        return pltpu.make_async_remote_copy(
            src_ref=xn.at[r, v, to_peer(d), rows, lanes], dst_ref=gath.at[r, v, slot, rows, lanes],
            send_sem=x_send.at[r, v, d - 1, pc, hh], recv_sem=x_recv.at[r, v, d - 1, pc, hh],
            device_id=(s, to_peer(d)), device_id_type=MESH)

    def a_copy(r, v, d, pc, hh, landing=False):
        slot = from_peer(d) if landing else f
        rows, lanes = pl.ds(pc * half, half), pl.ds(hh * part * hs, part * hs)
        return pltpu.make_async_remote_copy(
            src_ref=att_out.at[r, v, to_peer(d), rows, lanes], dst_ref=att_in.at[r, v, slot, rows, lanes],
            send_sem=a_send.at[r, v, d - 1, pc, hh], recv_sem=a_recv.at[r, v, d - 1, pc, hh],
            device_id=(s, to_peer(d)), device_id_type=MESH)

    def m_copy(d, landing=False):
        slot = from_peer(d) if landing else f
        return pltpu.make_async_remote_copy(
            src_ref=wm_all.at[f], dst_ref=wm_all.at[slot],
            send_sem=m_send.at[d - 1], recv_sem=m_recv.at[d - 1],
            device_id=(s, to_peer(d)), device_id_type=MESH)

    def s_copy(r, v, pc, landing=False):
        at = v if landing else lax.rem(v + jnp.where(s == segments - 1, 1, 0), virtual)
        target = out if r == ROUNDS - 1 else st_in.at[r]
        rows = pl.ds(pc * half, half)
        return pltpu.make_async_remote_copy(
            src_ref=st_out.at[r, v, rows], dst_ref=target.at[at, rows],
            send_sem=s_send.at[r, v, pc], recv_sem=s_recv.at[r, at, pc],
            device_id=(ahead, f), device_id_type=MESH)

    def state_of(r):
        return stream if r == 0 else st_in.at[r - 1]

    def order(r):
        if r == 0:
            return list(range(virtual))
        return [lax.rem(o + jnp.where(s < r, 1, 0), virtual) for o in range(virtual)]

    def norm(r, v, pc):
        state = state_of(r)

        def rows_body(i, carry):
            rows = pl.ds(pl.multiple_of(pc * half + i * 16, 16), 16)
            total = jnp.zeros((16, LANES), F32)
            for c in range(width // LANES):
                wide = state[v, rows, c * LANES:(c + 1) * LANES].astype(F32)
                total = total + wide * wide
            scale = lax.rsqrt(jnp.sum(total, axis=1, keepdims=True) / width + EPS)
            for c in range(heads):
                wide = state[v, rows, c * hs:(c + 1) * hs].astype(F32)
                g = gain[v, :, c * hs:(c + 1) * hs]
                j, at = c // local_heads, (c % local_heads) * hs
                xn[r, v, j, rows, at:at + hs] = (wide * scale * g).astype(BF16)
            return carry

        lax.fori_loop(0, half // 16, rows_body, 0)

    def count_blocks():
        lane_block = lax.broadcasted_iota(jnp.int32, (BLK, seq), 1) // BLK
        for v in range(virtual):
            for i in range(blocks):
                window = [(i - 1) % blocks, i, (i + 1) % blocks, 0]
                total = jnp.zeros((BLK, seq), F32)
                for b in window:
                    total = total + jnp.where(lane_block == b, 1.0, 0.0)
                for k in range(randoms):
                    total = total + jnp.where(lane_block == ids[v, i, k], 1.0, 0.0)
                counts[v, i * BLK:(i + 1) * BLK, :] = total

    def attention(r, v, hh):
        step = 4 if part % 4 == 0 else 1

        def one_head(h):
            lanes = pl.ds(pl.multiple_of(h * hs, hs), hs)
            x = gath[r, v, :, :, lanes].reshape(seq, hs)
            q = (jnp.dot(x, wq[v, h], preferred_element_type=F32) * hs ** (-0.5)).astype(BF16)
            k = jnp.dot(x, wk[v, h], preferred_element_type=F32).astype(BF16)
            val = jnp.dot(x, wv[v, h], preferred_element_type=F32).astype(BF16)
            scores = lax.dot_general(q, k, (((1,), (1,)), ((), ())), preferred_element_type=F32)
            count = counts[v]
            scores = jnp.where(count > 0.0, scores, -3e38)
            powers = jnp.exp(scores - jnp.max(scores, axis=1, keepdims=True)) * count
            weights = (powers * (1.0 / jnp.sum(powers, axis=1, keepdims=True))).astype(BF16)
            att = jnp.dot(weights, val, preferred_element_type=F32).astype(BF16)
            att_out[r, v, :, :, lanes] = att.reshape(peers, tokens, hs)

        def body(i, carry):
            for u in range(step):
                one_head(hh * part + i * step + u)
            return carry

        lax.fori_loop(0, part // step, body, 0)

    def pack_mix():
        def body(i, carry):
            rows = pl.ds(pl.multiple_of(i * LANES, LANES), LANES)
            both = [wm[v, rows, :].astype(F32) for v in range(virtual)]
            wm_all[f, rows, :] = jnp.concatenate(both, axis=1).astype(BF16)
            return carry

        lax.fori_loop(0, heads * heads // LANES, body, 0)

    def spread_mix():
        def body(i, carry):
            rows = pl.ds(pl.multiple_of(i * LANES, LANES), LANES)
            each = [wm_all[j, rows, :].astype(F32) for j in range(peers)]
            for v in range(virtual):
                wm_t[v, rows, :] = jnp.concatenate(
                    [e[:, v * local:(v + 1) * local] for e in each], axis=1)
            return carry

        lax.fori_loop(0, heads * heads // LANES, body, 0)

    def mix(r, v, pc):
        state = state_of(r)
        on = jnp.full((half, hs), live[v].astype(F32))

        rows = pl.ds(pc * half, half)

        def body(group, carry):
            sums = [jnp.zeros((half, hs), F32) for _ in range(8)]
            for h in range(heads):
                j, at = h // local_heads, (h % local_heads) * hs
                a = att_in[r, v, j, rows, at:at + hs].astype(F32)
                w = wm_t[v, pl.ds(pl.multiple_of(h * heads + group * 8, 8), 8), :]
                for g in range(8):
                    sums[g] = sums[g] + a * w[g:g + 1]
            for g in range(8):
                lanes = pl.ds(pl.multiple_of((group * 8 + g) * hs, hs), hs)
                wide = state[v, rows, lanes].astype(F32)
                updated = wide + sums[g].astype(BF16).astype(F32)
                st_out[r, v, rows, lanes] = jnp.where(on > 0.0, updated, wide).astype(BF16)
            return carry

        lax.fori_loop(0, heads // 8, body, 0)

    others = range(1, peers)
    pieces = range(PIECES)
    def send_x(r, v, pc):
        for hh in pieces:
            for d in others:
                x_copy(r, v, d, pc, hh).start()

    def send_a(r, v, hh):
        for pc in pieces:
            for d in others:
                a_copy(r, v, d, pc, hh).start()

    def wait_x(r, v, hh):
        for d in others:
            for pc in pieces:
                x_copy(r, v, d, pc, hh, landing=True).wait_recv()

    def wait_a(r, v, pc):
        for d in others:
            for hh in pieces:
                a_copy(r, v, d, pc, hh, landing=True).wait_recv()

    for r in range(ROUNDS):
        todo = order(r)
        for o, v in enumerate(todo):
            if r == 0:
                load(0, v).wait()
                gain[v] = gain_in[v:v + 1, :].astype(F32)
            for pc in pieces:
                if r > 0:
                    s_copy(r - 1, v, pc, landing=True).wait_recv()
                norm(r, v, pc)
                if r == 0 and o == 0 and pc == 0:
                    pl.semaphore_wait(barrier, peers + 1)
                if o == 0:
                    send_x(r, v, pc)
            gath[r, v, f] = xn[r, v, f]
        if r == 0:
            pack_mix()
            count_blocks()
        for o, v in enumerate(todo):
            if r == 0:
                for n in range(1, 4):
                    load(n, v).wait()
            for hh in pieces:
                wait_x(r, v, hh)
                if hh == 0:
                    if o + 1 < virtual:
                        for pc in pieces:
                            send_x(r, todo[o + 1], pc)
                    if r == 0 and o == 0:
                        for d in others:
                            m_copy(d).start()
                attention(r, v, hh)
                if o == 0:
                    send_a(r, v, hh)
            att_in[r, v, f] = att_out[r, v, f]
        if r == 0:
            for d in others:
                m_copy(d, landing=True).wait_recv()
            spread_mix()
        for o, v in enumerate(todo):
            for pc in pieces:
                wait_a(r, v, pc)
                if pc == 0 and o + 1 < virtual:
                    for hh in pieces:
                        send_a(r, todo[o + 1], hh)
                mix(r, v, pc)
                s_copy(r, v, pc).start()

    for v in range(virtual):
        for pc in pieces:
            s_copy(ROUNDS - 1, v, pc, landing=True).wait_recv()
    for r in range(ROUNDS):
        for v in range(virtual):
            for pc in pieces:
                for d in others:
                    for hh in pieces:
                        x_copy(r, v, d, pc, hh).wait_send()
                        a_copy(r, v, d, pc, hh).wait_send()
                s_copy(r, v, pc).wait_send()
    for d in others:
        m_copy(d).wait_send()


def shards(segments, peers, stream, gain, w_query, w_key, w_value, w_mix, active, random_blocks):
    virtual, _, tokens, width = stream.shape
    local_heads, hs = w_query.shape[2], w_query.shape[3]
    heads = width // hs
    local = w_mix.shape[2]
    seq = tokens * peers
    group = local_heads * hs
    vmem = pl.BlockSpec(memory_space=pltpu.VMEM)
    hbm = pl.BlockSpec(memory_space=pl.ANY)
    smem = pl.BlockSpec(memory_space=pltpu.SMEM)
    dma = pltpu.SemaphoreType.DMA
    apart = max(peers - 1, 1)
    result = pl.pallas_call(
        functools.partial(kernel, segments, peers),
        out_shape=jax.ShapeDtypeStruct((virtual, tokens, width), BF16),
        in_specs=[hbm, vmem, hbm, hbm, hbm, vmem, smem, smem],
        out_specs=pl.BlockSpec(memory_space=pl.ANY),
        scratch_shapes=[
            pltpu.VMEM((virtual, tokens, width), BF16),
            pltpu.VMEM((virtual, 1, width), F32),
            pltpu.VMEM((virtual, local_heads, hs, hs), BF16),
            pltpu.VMEM((virtual, local_heads, hs, hs), BF16),
            pltpu.VMEM((virtual, local_heads, hs, hs), BF16),
            pltpu.VMEM((max(ROUNDS - 1, 1), virtual, tokens, width), BF16),
            pltpu.VMEM((ROUNDS, virtual, peers, tokens, group), BF16),
            pltpu.VMEM((ROUNDS, virtual, peers, tokens, group), BF16),
            pltpu.VMEM((ROUNDS, virtual, peers, tokens, group), BF16),
            pltpu.VMEM((ROUNDS, virtual, peers, tokens, group), BF16),
            pltpu.VMEM((ROUNDS, virtual, tokens, width), BF16),
            pltpu.VMEM((peers, heads * heads, virtual * local), BF16),
            pltpu.VMEM((virtual, heads * heads, hs), F32),
            pltpu.VMEM((virtual, seq, seq), F32),
            dma((ROUNDS, virtual, apart, PIECES, PIECES)),
            dma((ROUNDS, virtual, apart, PIECES, PIECES)),
            dma((ROUNDS, virtual, apart, PIECES, PIECES)),
            dma((ROUNDS, virtual, apart, PIECES, PIECES)),
            dma((ROUNDS, virtual, PIECES)),
            dma((ROUNDS, virtual, PIECES)),
            dma((apart,)),
            dma((apart,)),
            dma((4, virtual)),
        ],
        compiler_params=pltpu.CompilerParams(
            collective_id=0, has_side_effects=True, vmem_limit_bytes=56 * 1024 * 1024
        ),
        cost_estimate=pl.CostEstimate(
            flops=ROUNDS * virtual * seq * local_heads * hs * (6 * hs + 4 * seq),
            bytes_accessed=6 * 1024 * 1024,
            transcendentals=ROUNDS * virtual * seq * local_heads * seq,
        ),
    )(
        stream[:, 0],
        gain[:, 0],
        w_query[:, 0],
        w_key[:, 0],
        w_value[:, 0],
        w_mix[:, 0].transpose(0, 2, 3, 1).reshape(virtual, heads * heads, local),
        active[:, 0],
        random_blocks[:, 0],
    )
    return result[:, None]


def solution(mesh):
    in_specs = (
        P(None, "segment", "fsdp", None),
        P(None, "segment", None),
        P(None, "segment", "fsdp", None, None),
        P(None, "segment", "fsdp", None, None),
        P(None, "segment", "fsdp", None, None),
        P(None, "segment", "fsdp", None, None),
        P(None, "segment"),
        P(None, "segment", None, None),
    )
    out_specs = P(None, "segment", "fsdp", None)
    body = functools.partial(shards, mesh.shape["segment"], mesh.shape["fsdp"])
    return jax.shard_map(body, mesh=mesh, in_specs=in_specs, out_specs=out_specs, check_vma=False)
```

```python
import functools

import jax
import jax.numpy as jnp
from jax import lax
from jax.experimental import pallas as pl
from jax.experimental.pallas import tpu as pltpu
from jax.sharding import PartitionSpec as P

BLK = 64
ROUNDS = 2
EPS = 1e-05
LANES = 128
PIECES = 2
MESH = pl.DeviceIdType.MESH
F32 = jnp.float32
BF16 = jnp.bfloat16


def kernel(
    segments, peers, stream_hbm, gain_in, wq_hbm, wk_hbm, wv_hbm, wm, live, ids, out,
    stream, gain, wq, wk, wv,
    st_in, xn, gath, att_out, att_in, st_out, wm_all, wm_t, counts,
    x_send, x_recv, a_send, a_recv, s_send, s_recv, m_send, m_recv, load_sem,
):
    virtual, tokens, width = stream.shape
    local_heads, hs = wq.shape[1], wq.shape[2]
    half = tokens // PIECES
    part = local_heads // PIECES
    local = wm.shape[2]
    heads = width // hs
    seq = tokens * peers
    blocks = seq // BLK
    randoms = ids.shape[2]
    s = lax.axis_index("segment")
    f = lax.axis_index("fsdp")
    ahead = lax.rem(s + 1, segments)
    behind = lax.rem(s + segments - 1, segments)

    barrier = pltpu.get_barrier_semaphore()
    for d in range(1, peers):
        pl.semaphore_signal(barrier, inc=1, device_id=(s, lax.rem(f + d, peers)), device_id_type=MESH)
    for other in (ahead, behind):
        pl.semaphore_signal(barrier, inc=1, device_id=(other, f), device_id_type=MESH)

    def load(n, v):
        source, target = ((stream_hbm, stream), (wq_hbm, wq), (wk_hbm, wk), (wv_hbm, wv))[n]
        return pltpu.make_async_copy(source.at[v], target.at[v], load_sem.at[n, v])

    for n in range(4):
        for v in range(virtual):
            load(n, v).start()

    def to_peer(d):
        return lax.rem(f + d, peers)

    def from_peer(d):
        return lax.rem(f + peers - d, peers)

    def x_copy(r, v, d, pc, hh, landing=False):
        slot = from_peer(d) if landing else f
        rows, lanes = pl.ds(pc * half, half), pl.ds(hh * part * hs, part * hs)
        return pltpu.make_async_remote_copy(
            src_ref=xn.at[r, v, to_peer(d), rows, lanes], dst_ref=gath.at[r, v, slot, rows, lanes],
            send_sem=x_send.at[r, v, d - 1, pc, hh], recv_sem=x_recv.at[r, v, d - 1, pc, hh],
            device_id=(s, to_peer(d)), device_id_type=MESH)

    def a_copy(r, v, d, pc, hh, landing=False):
        slot = from_peer(d) if landing else f
        rows, lanes = pl.ds(pc * half, half), pl.ds(hh * part * hs, part * hs)
        return pltpu.make_async_remote_copy(
            src_ref=att_out.at[r, v, to_peer(d), rows, lanes], dst_ref=att_in.at[r, v, slot, rows, lanes],
            send_sem=a_send.at[r, v, d - 1, pc, hh], recv_sem=a_recv.at[r, v, d - 1, pc, hh],
            device_id=(s, to_peer(d)), device_id_type=MESH)

    def m_copy(d, landing=False):
        slot = from_peer(d) if landing else f
        return pltpu.make_async_remote_copy(
            src_ref=wm_all.at[f], dst_ref=wm_all.at[slot],
            send_sem=m_send.at[d - 1], recv_sem=m_recv.at[d - 1],
            device_id=(s, to_peer(d)), device_id_type=MESH)

    def s_copy(r, v, pc, landing=False):
        at = v if landing else lax.rem(v + jnp.where(s == segments - 1, 1, 0), virtual)
        target = out if r == ROUNDS - 1 else st_in.at[r]
        rows = pl.ds(pc * half, half)
        return pltpu.make_async_remote_copy(
            src_ref=st_out.at[r, v, rows], dst_ref=target.at[at, rows],
            send_sem=s_send.at[r, v, pc], recv_sem=s_recv.at[r, at, pc],
            device_id=(ahead, f), device_id_type=MESH)

    def state_of(r):
        return stream if r == 0 else st_in.at[r - 1]

    def order(r):
        if r == 0:
            return list(range(virtual))
        return [lax.rem(o + jnp.where(s < r, 1, 0), virtual) for o in range(virtual)]

    def norm(r, v, pc):
        state = state_of(r)

        def rows_body(i, carry):
            rows = pl.ds(pl.multiple_of(pc * half + i * 16, 16), 16)
            total = jnp.zeros((16, LANES), F32)
            for c in range(width // LANES):
                wide = state[v, rows, c * LANES:(c + 1) * LANES].astype(F32)
                total = total + wide * wide
            scale = lax.rsqrt(jnp.sum(total, axis=1, keepdims=True) / width + EPS)
            for c in range(heads):
                wide = state[v, rows, c * hs:(c + 1) * hs].astype(F32)
                g = gain[v, :, c * hs:(c + 1) * hs]
                j, at = c // local_heads, (c % local_heads) * hs
                xn[r, v, j, rows, at:at + hs] = (wide * scale * g).astype(BF16)
            return carry

        lax.fori_loop(0, half // 16, rows_body, 0)

    def count_blocks():
        lane_block = lax.broadcasted_iota(jnp.int32, (BLK, seq), 1) // BLK
        for v in range(virtual):
            for i in range(blocks):
                window = [(i - 1) % blocks, i, (i + 1) % blocks, 0]
                total = jnp.zeros((BLK, seq), F32)
                for b in window:
                    total = total + jnp.where(lane_block == b, 1.0, 0.0)
                for k in range(randoms):
                    total = total + jnp.where(lane_block == ids[v, i, k], 1.0, 0.0)
                counts[v, i * BLK:(i + 1) * BLK, :] = total

    def attention(r, v, hh):
        step = 4 if part % 4 == 0 else 1

        ones = jnp.ones((seq, hs), BF16)

        def body(i, carry):
            mine = [hh * part + i * step + u for u in range(step)]
            lanes = [pl.ds(pl.multiple_of(h * hs, hs), hs) for h in mine]
            x = [gath[r, v, :, :, at].reshape(seq, hs) for at in lanes]
            qk = [
                jnp.dot(x[u], jnp.concatenate([wq[v, h], wk[v, h]], axis=1), preferred_element_type=F32)
                for u, h in enumerate(mine)
            ]
            q = [(a[:, :hs] * hs ** (-0.5)).astype(BF16) for a in qk]
            k = [a[:, hs:].astype(BF16) for a in qk]
            scores = [
                lax.dot_general(a, b, (((1,), (1,)), ((), ())), preferred_element_type=F32)
                for a, b in zip(q, k)
            ]
            val = [
                jnp.dot(x[u], wv[v, h], preferred_element_type=F32).astype(BF16)
                for u, h in enumerate(mine)
            ]
            count = counts[v]
            if blocks > 3:
                scores = [jnp.where(count > 0.0, a, -3e38) for a in scores]
            top = [jnp.max(a, axis=1, keepdims=True) for a in scores]
            powers = [(jnp.exp(a - m) * count).astype(BF16) for a, m in zip(scores, top)]
            sums = [
                jnp.dot(p, jnp.concatenate([a, ones], axis=1), preferred_element_type=F32)
                for p, a in zip(powers, val)
            ]
            att = [(a[:, :hs] * (1.0 / a[:, hs:])).astype(BF16) for a in sums]
            for at, a in zip(lanes, att):
                att_out[r, v, :, :, at] = a.reshape(peers, tokens, hs)
            return carry

        lax.fori_loop(0, part // step, body, 0)

    def pack_mix():
        def body(i, carry):
            rows = pl.ds(pl.multiple_of(i * LANES, LANES), LANES)
            both = [wm[v, rows, :].astype(F32) for v in range(virtual)]
            wm_all[f, rows, :] = jnp.concatenate(both, axis=1).astype(BF16)
            return carry

        lax.fori_loop(0, heads * heads // LANES, body, 0)

    def spread_mix():
        def body(i, carry):
            rows = pl.ds(pl.multiple_of(i * LANES, LANES), LANES)
            each = [wm_all[j, rows, :].astype(F32) for j in range(peers)]
            for v in range(virtual):
                wm_t[v, rows, :] = jnp.concatenate(
                    [e[:, v * local:(v + 1) * local] for e in each], axis=1)
            return carry

        lax.fori_loop(0, heads * heads // LANES, body, 0)

    def mix(r, v, pc):
        state = state_of(r)
        on = jnp.full((half, hs), live[v].astype(F32))

        rows = pl.ds(pc * half, half)

        def body(group, carry):
            sums = [jnp.zeros((half, hs), F32) for _ in range(8)]
            for h in range(heads):
                j, at = h // local_heads, (h % local_heads) * hs
                a = att_in[r, v, j, rows, at:at + hs].astype(F32)
                w = wm_t[v, pl.ds(pl.multiple_of(h * heads + group * 8, 8), 8), :]
                for g in range(8):
                    sums[g] = sums[g] + a * w[g:g + 1]
            for g in range(8):
                lanes = pl.ds(pl.multiple_of((group * 8 + g) * hs, hs), hs)
                wide = state[v, rows, lanes].astype(F32)
                updated = wide + sums[g].astype(BF16).astype(F32)
                st_out[r, v, rows, lanes] = jnp.where(on > 0.0, updated, wide).astype(BF16)
            return carry

        lax.fori_loop(0, heads // 8, body, 0)

    others = range(1, peers)
    pieces = range(PIECES)
    def send_x(r, v, pc):
        for hh in pieces:
            for d in others:
                x_copy(r, v, d, pc, hh).start()

    def send_a(r, v, hh):
        for pc in pieces:
            for d in others:
                a_copy(r, v, d, pc, hh).start()

    def wait_x(r, v, hh):
        for d in others:
            for pc in pieces:
                x_copy(r, v, d, pc, hh, landing=True).wait_recv()

    def wait_a(r, v, pc):
        for d in others:
            for hh in pieces:
                a_copy(r, v, d, pc, hh, landing=True).wait_recv()

    for r in range(ROUNDS):
        todo = order(r)
        for o, v in enumerate(todo):
            if r == 0:
                load(0, v).wait()
                gain[v] = gain_in[v:v + 1, :].astype(F32)
            for pc in pieces:
                if r > 0:
                    s_copy(r - 1, v, pc, landing=True).wait_recv()
                norm(r, v, pc)
                if r == 0 and o == 0 and pc == 0:
                    pl.semaphore_wait(barrier, peers + 1)
                if o == 0:
                    send_x(r, v, pc)
            gath[r, v, f] = xn[r, v, f]
        if r == 0:
            pack_mix()
            count_blocks()
        for o, v in enumerate(todo):
            if r == 0:
                for n in range(1, 4):
                    load(n, v).wait()
            for hh in pieces:
                wait_x(r, v, hh)
                if hh == 0:
                    if o + 1 < virtual:
                        for pc in pieces:
                            send_x(r, todo[o + 1], pc)
                    if r == 0 and o == 0:
                        for d in others:
                            m_copy(d).start()
                attention(r, v, hh)
                if o == 0:
                    send_a(r, v, hh)
            att_in[r, v, f] = att_out[r, v, f]
        if r == 0:
            for d in others:
                m_copy(d, landing=True).wait_recv()
            spread_mix()
        for o, v in enumerate(todo):
            for pc in pieces:
                wait_a(r, v, pc)
                if pc == 0 and o + 1 < virtual:
                    for hh in pieces:
                        send_a(r, todo[o + 1], hh)
                mix(r, v, pc)
                s_copy(r, v, pc).start()

    for v in range(virtual):
        for pc in pieces:
            s_copy(ROUNDS - 1, v, pc, landing=True).wait_recv()
    for r in range(ROUNDS):
        for v in range(virtual):
            for pc in pieces:
                for d in others:
                    for hh in pieces:
                        x_copy(r, v, d, pc, hh).wait_send()
                        a_copy(r, v, d, pc, hh).wait_send()
                s_copy(r, v, pc).wait_send()
    for d in others:
        m_copy(d).wait_send()


def shards(segments, peers, stream, gain, w_query, w_key, w_value, w_mix, active, random_blocks):
    virtual, _, tokens, width = stream.shape
    local_heads, hs = w_query.shape[2], w_query.shape[3]
    heads = width // hs
    local = w_mix.shape[2]
    seq = tokens * peers
    group = local_heads * hs
    vmem = pl.BlockSpec(memory_space=pltpu.VMEM)
    hbm = pl.BlockSpec(memory_space=pl.ANY)
    smem = pl.BlockSpec(memory_space=pltpu.SMEM)
    dma = pltpu.SemaphoreType.DMA
    apart = max(peers - 1, 1)
    result = pl.pallas_call(
        functools.partial(kernel, segments, peers),
        out_shape=jax.ShapeDtypeStruct((virtual, tokens, width), BF16),
        in_specs=[hbm, vmem, hbm, hbm, hbm, vmem, smem, smem],
        out_specs=pl.BlockSpec(memory_space=pl.ANY),
        scratch_shapes=[
            pltpu.VMEM((virtual, tokens, width), BF16),
            pltpu.VMEM((virtual, 1, width), F32),
            pltpu.VMEM((virtual, local_heads, hs, hs), BF16),
            pltpu.VMEM((virtual, local_heads, hs, hs), BF16),
            pltpu.VMEM((virtual, local_heads, hs, hs), BF16),
            pltpu.VMEM((max(ROUNDS - 1, 1), virtual, tokens, width), BF16),
            pltpu.VMEM((ROUNDS, virtual, peers, tokens, group), BF16),
            pltpu.VMEM((ROUNDS, virtual, peers, tokens, group), BF16),
            pltpu.VMEM((ROUNDS, virtual, peers, tokens, group), BF16),
            pltpu.VMEM((ROUNDS, virtual, peers, tokens, group), BF16),
            pltpu.VMEM((ROUNDS, virtual, tokens, width), BF16),
            pltpu.VMEM((peers, heads * heads, virtual * local), BF16),
            pltpu.VMEM((virtual, heads * heads, hs), F32),
            pltpu.VMEM((virtual, seq, seq), F32),
            dma((ROUNDS, virtual, apart, PIECES, PIECES)),
            dma((ROUNDS, virtual, apart, PIECES, PIECES)),
            dma((ROUNDS, virtual, apart, PIECES, PIECES)),
            dma((ROUNDS, virtual, apart, PIECES, PIECES)),
            dma((ROUNDS, virtual, PIECES)),
            dma((ROUNDS, virtual, PIECES)),
            dma((apart,)),
            dma((apart,)),
            dma((4, virtual)),
        ],
        compiler_params=pltpu.CompilerParams(
            collective_id=0, has_side_effects=True, vmem_limit_bytes=56 * 1024 * 1024
        ),
        cost_estimate=pl.CostEstimate(
            flops=ROUNDS * virtual * seq * local_heads * hs * (6 * hs + 4 * seq),
            bytes_accessed=6 * 1024 * 1024,
            transcendentals=ROUNDS * virtual * seq * local_heads * seq,
        ),
    )(
        stream[:, 0],
        gain[:, 0],
        w_query[:, 0],
        w_key[:, 0],
        w_value[:, 0],
        w_mix[:, 0].transpose(0, 2, 3, 1).reshape(virtual, heads * heads, local),
        active[:, 0],
        random_blocks[:, 0],
    )
    return result[:, None]


def solution(mesh):
    in_specs = (
        P(None, "segment", "fsdp", None),
        P(None, "segment", None),
        P(None, "segment", "fsdp", None, None),
        P(None, "segment", "fsdp", None, None),
        P(None, "segment", "fsdp", None, None),
        P(None, "segment", "fsdp", None, None),
        P(None, "segment"),
        P(None, "segment", None, None),
    )
    out_specs = P(None, "segment", "fsdp", None)
    body = functools.partial(shards, mesh.shape["segment"], mesh.shape["fsdp"])
    return jax.shard_map(body, mesh=mesh, in_specs=in_specs, out_specs=out_specs, check_vma=False)
```

```python
import functools

import jax
import jax.numpy as jnp
from jax import lax
from jax.experimental import pallas as pl
from jax.experimental.pallas import tpu as pltpu
from jax.sharding import PartitionSpec as P

BLK = 64
ROUNDS = 2
EPS = 1e-05
LANES = 128
PIECES = 2
MESH = pl.DeviceIdType.MESH
F32 = jnp.float32
BF16 = jnp.bfloat16


def kernel(
    segments, peers, stream_hbm, gain_in, wq_hbm, wk_hbm, wv_hbm, wm, live, ids, out,
    stream, gain, wq, wk, wv,
    st_in, xn, gath, att_out, att_in, st_out, wm_all, wm_t, counts, st_ahead, wm_behind, wm_last,
    x_send, x_recv, a_send, a_recv, s_send, s_recv, m_send, m_recv, load_sem,
    w_send, w_recv, store_sem,
):
    virtual, tokens, width = stream.shape
    local_heads, hs = wq.shape[1], wq.shape[2]
    half = tokens // PIECES
    part = local_heads // PIECES
    local = wm.shape[2]
    heads = width // hs
    seq = tokens * peers
    blocks = seq // BLK
    randoms = ids.shape[2]
    s = lax.axis_index("segment")
    f = lax.axis_index("fsdp")
    ahead = lax.rem(s + 1, segments)
    behind = lax.rem(s + segments - 1, segments)

    barrier = pltpu.get_barrier_semaphore()
    for d in range(1, peers):
        pl.semaphore_signal(barrier, inc=1, device_id=(s, lax.rem(f + d, peers)), device_id_type=MESH)
    for d in range(peers):
        pl.semaphore_signal(barrier, inc=1, device_id=(behind, lax.rem(f + d, peers)), device_id_type=MESH)
    everyone = 2 * peers - 1

    def load(n, v):
        source, target = ((stream_hbm, stream), (wq_hbm, wq), (wk_hbm, wk), (wv_hbm, wv))[n]
        return pltpu.make_async_copy(source.at[v], target.at[v], load_sem.at[n, v])

    for n in range(4):
        for v in range(virtual):
            load(n, v).start()

    def to_peer(d):
        return lax.rem(f + d, peers)

    def from_peer(d):
        return lax.rem(f + peers - d, peers)

    def x_copy(r, v, d, pc, hh, landing=False):
        slot = from_peer(d) if landing else f
        rows, lanes = pl.ds(pc * half, half), pl.ds(hh * part * hs, part * hs)
        return pltpu.make_async_remote_copy(
            src_ref=xn.at[r, v, to_peer(d), rows, lanes], dst_ref=gath.at[r, v, slot, rows, lanes],
            send_sem=x_send.at[r, v, d - 1, pc, hh], recv_sem=x_recv.at[r, v, d - 1, pc, hh],
            device_id=(s, to_peer(d)), device_id_type=MESH)

    def onward(v):
        return lax.rem(v + jnp.where(s == segments - 1, 1, 0), virtual)

    def a_copy(r, v, d, pc, hh, landing=False):
        last = r == ROUNDS - 1
        slot = from_peer(d) if landing else f
        at = onward(v) if last and not landing else v
        rows, lanes = pl.ds(pc * half, half), pl.ds(hh * part * hs, part * hs)
        return pltpu.make_async_remote_copy(
            src_ref=att_out.at[r, v, to_peer(d), rows, lanes], dst_ref=att_in.at[r, at, slot, rows, lanes],
            send_sem=a_send.at[r, v, d, pc, hh], recv_sem=a_recv.at[r, at, d, pc, hh],
            device_id=(ahead if last else s, to_peer(d)), device_id_type=MESH)

    def m_copy(d, landing=False):
        slot = from_peer(d) if landing else f
        return pltpu.make_async_remote_copy(
            src_ref=wm_all.at[f], dst_ref=wm_all.at[slot],
            send_sem=m_send.at[d - 1], recv_sem=m_recv.at[d - 1],
            device_id=(s, to_peer(d)), device_id_type=MESH)

    def s_copy(r, v, pc, landing=False):
        at = v if landing else onward(v)
        rows = pl.ds(pc * half, half)
        return pltpu.make_async_remote_copy(
            src_ref=st_out.at[r, v, rows], dst_ref=st_in.at[r, at, rows],
            send_sem=s_send.at[r, v, pc], recv_sem=s_recv.at[r, at, pc],
            device_id=(ahead, f), device_id_type=MESH)

    def forward_copy(v, pc, landing=False):
        at = v if landing else onward(v)
        rows = pl.ds(pc * half, half)
        return pltpu.make_async_remote_copy(
            src_ref=st_in.at[ROUNDS - 2, v, rows], dst_ref=st_ahead.at[at, rows],
            send_sem=s_send.at[ROUNDS - 1, v, pc], recv_sem=s_recv.at[ROUNDS - 1, at, pc],
            device_id=(ahead, f), device_id_type=MESH)

    def w_copy():
        return pltpu.make_async_remote_copy(
            src_ref=wm_all, dst_ref=wm_behind, send_sem=w_send.at[0], recv_sem=w_recv.at[0],
            device_id=(ahead, f), device_id_type=MESH)

    def store(v, pc):
        rows = pl.ds(pc * half, half)
        return pltpu.make_async_copy(
            st_out.at[ROUNDS - 1, v, rows], out.at[v, rows], store_sem.at[v, pc])

    def state_of(r):
        return stream if r == 0 else st_in.at[r - 1]

    def order(r):
        if r == 0:
            return list(range(virtual))
        return [lax.rem(o + jnp.where(s < r, 1, 0), virtual) for o in range(virtual)]

    def norm(r, v, pc):
        state = state_of(r)

        def rows_body(i, carry):
            rows = pl.ds(pl.multiple_of(pc * half + i * 16, 16), 16)
            total = jnp.zeros((16, LANES), F32)
            for c in range(width // LANES):
                wide = state[v, rows, c * LANES:(c + 1) * LANES].astype(F32)
                total = total + wide * wide
            scale = lax.rsqrt(jnp.sum(total, axis=1, keepdims=True) / width + EPS)
            for c in range(heads):
                wide = state[v, rows, c * hs:(c + 1) * hs].astype(F32)
                g = gain[v, :, c * hs:(c + 1) * hs]
                j, at = c // local_heads, (c % local_heads) * hs
                xn[r, v, j, rows, at:at + hs] = (wide * scale * g).astype(BF16)
            return carry

        lax.fori_loop(0, half // 16, rows_body, 0)

    def count_blocks():
        lane_block = lax.broadcasted_iota(jnp.int32, (BLK, seq), 1) // BLK
        for v in range(virtual):
            for i in range(blocks):
                window = [(i - 1) % blocks, i, (i + 1) % blocks, 0]
                total = jnp.zeros((BLK, seq), F32)
                for b in window:
                    total = total + jnp.where(lane_block == b, 1.0, 0.0)
                for k in range(randoms):
                    total = total + jnp.where(lane_block == ids[v, i, k], 1.0, 0.0)
                counts[v, i * BLK:(i + 1) * BLK, :] = total

    def attention(r, v, hh):
        step = 4 if part % 4 == 0 else 1

        ones = jnp.ones((seq, hs), BF16)

        def body(i, carry):
            mine = [hh * part + i * step + u for u in range(step)]
            lanes = [pl.ds(pl.multiple_of(h * hs, hs), hs) for h in mine]
            x = [gath[r, v, :, :, at].reshape(seq, hs) for at in lanes]
            qk = [
                jnp.dot(x[u], jnp.concatenate([wq[v, h], wk[v, h]], axis=1), preferred_element_type=F32)
                for u, h in enumerate(mine)
            ]
            q = [(a[:, :hs] * hs ** (-0.5)).astype(BF16) for a in qk]
            k = [a[:, hs:].astype(BF16) for a in qk]
            scores = [
                lax.dot_general(a, b, (((1,), (1,)), ((), ())), preferred_element_type=F32)
                for a, b in zip(q, k)
            ]
            val = [
                jnp.dot(x[u], wv[v, h], preferred_element_type=F32).astype(BF16)
                for u, h in enumerate(mine)
            ]
            count = counts[v]
            if blocks > 3:
                scores = [jnp.where(count > 0.0, a, -3e38) for a in scores]
            top = [jnp.max(a, axis=1, keepdims=True) for a in scores]
            powers = [(jnp.exp(a - m) * count).astype(BF16) for a, m in zip(scores, top)]
            sums = [
                jnp.dot(p, jnp.concatenate([a, ones], axis=1), preferred_element_type=F32)
                for p, a in zip(powers, val)
            ]
            att = [(a[:, :hs] * (1.0 / a[:, hs:])).astype(BF16) for a in sums]
            for at, a in zip(lanes, att):
                att_out[r, v, :, :, at] = a.reshape(peers, tokens, hs)
            return carry

        lax.fori_loop(0, part // step, body, 0)

    def pack_mix():
        on = [jnp.where(live[v] > 0, 1.0, 0.0).astype(F32) for v in range(virtual)]

        def body(i, carry):
            rows = pl.ds(pl.multiple_of(i * LANES, LANES), LANES)
            both = [wm[v, rows, :].astype(F32) * on[v] for v in range(virtual)]
            wm_all[f, rows, :] = jnp.concatenate(both, axis=1).astype(BF16)
            return carry

        lax.fori_loop(0, heads * heads // LANES, body, 0)

    def spread_mix(packed, spread, place):
        def body(i, carry):
            rows = pl.ds(pl.multiple_of(i * LANES, LANES), LANES)
            each = [packed[j, rows, :].astype(F32) for j in range(peers)]
            for v in range(virtual):
                spread[place(v), rows, :] = jnp.concatenate(
                    [e[:, v * local:(v + 1) * local] for e in each], axis=1)
            return carry

        lax.fori_loop(0, heads * heads // LANES, body, 0)

    def mix(r, v, pc):
        last = r == ROUNDS - 1
        state, maps = (st_ahead, wm_last) if last else (state_of(r), wm_t)
        rows = pl.ds(pc * half, half)

        def body(group, carry):
            sums = [jnp.zeros((half, hs), F32) for _ in range(8)]
            for h in range(heads):
                j, at = h // local_heads, (h % local_heads) * hs
                a = att_in[r, v, j, rows, at:at + hs].astype(F32)
                w = maps[v, pl.ds(pl.multiple_of(h * heads + group * 8, 8), 8), :]
                for g in range(8):
                    sums[g] = sums[g] + a * w[g:g + 1]
            for g in range(8):
                lanes = pl.ds(pl.multiple_of((group * 8 + g) * hs, hs), hs)
                wide = state[v, rows, lanes].astype(F32)
                st_out[r, v, rows, lanes] = (wide + sums[g].astype(BF16).astype(F32)).astype(BF16)
            return carry

        lax.fori_loop(0, heads // 8, body, 0)

    others = range(1, peers)
    pieces = range(PIECES)
    def send_x(r, v, pc):
        for hh in pieces:
            for d in others:
                x_copy(r, v, d, pc, hh).start()

    def receivers(r):
        return range(peers) if r == ROUNDS - 1 else others

    def send_a(r, v, hh):
        for pc in pieces:
            for d in receivers(r):
                a_copy(r, v, d, pc, hh).start()

    def wait_x(r, v, hh):
        for d in others:
            for pc in pieces:
                x_copy(r, v, d, pc, hh, landing=True).wait_recv()

    def wait_a(r, v, pc):
        for d in receivers(r):
            for hh in pieces:
                a_copy(r, v, d, pc, hh, landing=True).wait_recv()

    for r in range(ROUNDS):
        last = r == ROUNDS - 1
        todo = order(r)
        for o, v in enumerate(todo):
            if r == 0:
                load(0, v).wait()
                gain[v] = gain_in[v:v + 1, :].astype(F32)
            for pc in pieces:
                if r > 0:
                    s_copy(r - 1, v, pc, landing=True).wait_recv()
                norm(r, v, pc)
                if r == 0 and o == 0 and pc == 0:
                    pl.semaphore_wait(barrier, everyone)
                if o == 0:
                    send_x(r, v, pc)
                if last:
                    forward_copy(v, pc).start()
            gath[r, v, f] = xn[r, v, f]
        if r == 0:
            pack_mix()
            count_blocks()
        for o, v in enumerate(todo):
            if r == 0:
                for n in range(1, 4):
                    load(n, v).wait()
            for hh in pieces:
                wait_x(r, v, hh)
                if hh == 0:
                    if o + 1 < virtual:
                        for pc in pieces:
                            send_x(r, todo[o + 1], pc)
                    if r == 0 and o == 0:
                        for d in others:
                            m_copy(d).start()
                attention(r, v, hh)
                if o == 0 or last:
                    send_a(r, v, hh)
            if not last:
                att_in[r, v, f] = att_out[r, v, f]
        if r == 0:
            for d in others:
                m_copy(d, landing=True).wait_recv()
            w_copy().start()
            spread_mix(wm_all, wm_t, lambda v: v)
        if last:
            w_copy().wait_recv()
            spread_mix(wm_behind, wm_last, lambda v: lax.rem(v + jnp.where(s == 0, 1, 0), virtual))
        done = order(r + 1) if last else todo
        for o, v in enumerate(done):
            for pc in pieces:
                wait_a(r, v, pc)
                if last:
                    forward_copy(v, pc, landing=True).wait_recv()
                elif pc == 0 and o + 1 < virtual:
                    for hh in pieces:
                        send_a(r, done[o + 1], hh)
                mix(r, v, pc)
                if last:
                    store(v, pc).start()
                else:
                    s_copy(r, v, pc).start()

    for r in range(ROUNDS):
        last = r == ROUNDS - 1
        for v in range(virtual):
            for pc in pieces:
                for hh in pieces:
                    for d in others:
                        x_copy(r, v, d, pc, hh).wait_send()
                    for d in receivers(r):
                        a_copy(r, v, d, pc, hh).wait_send()
                if last:
                    forward_copy(v, pc).wait_send()
                    store(v, pc).wait()
                else:
                    s_copy(r, v, pc).wait_send()
    for d in others:
        m_copy(d).wait_send()
    w_copy().wait_send()


def shards(segments, peers, stream, gain, w_query, w_key, w_value, w_mix, active, random_blocks):
    virtual, _, tokens, width = stream.shape
    local_heads, hs = w_query.shape[2], w_query.shape[3]
    heads = width // hs
    local = w_mix.shape[2]
    seq = tokens * peers
    group = local_heads * hs
    vmem = pl.BlockSpec(memory_space=pltpu.VMEM)
    hbm = pl.BlockSpec(memory_space=pl.ANY)
    smem = pl.BlockSpec(memory_space=pltpu.SMEM)
    dma = pltpu.SemaphoreType.DMA
    apart = max(peers - 1, 1)
    result = pl.pallas_call(
        functools.partial(kernel, segments, peers),
        out_shape=jax.ShapeDtypeStruct((virtual, tokens, width), BF16),
        in_specs=[hbm, vmem, hbm, hbm, hbm, vmem, smem, smem],
        out_specs=pl.BlockSpec(memory_space=pl.ANY),
        scratch_shapes=[
            pltpu.VMEM((virtual, tokens, width), BF16),
            pltpu.VMEM((virtual, 1, width), F32),
            pltpu.VMEM((virtual, local_heads, hs, hs), BF16),
            pltpu.VMEM((virtual, local_heads, hs, hs), BF16),
            pltpu.VMEM((virtual, local_heads, hs, hs), BF16),
            pltpu.VMEM((max(ROUNDS - 1, 1), virtual, tokens, width), BF16),
            pltpu.VMEM((ROUNDS, virtual, peers, tokens, group), BF16),
            pltpu.VMEM((ROUNDS, virtual, peers, tokens, group), BF16),
            pltpu.VMEM((ROUNDS, virtual, peers, tokens, group), BF16),
            pltpu.VMEM((ROUNDS, virtual, peers, tokens, group), BF16),
            pltpu.VMEM((ROUNDS, virtual, tokens, width), BF16),
            pltpu.VMEM((peers, heads * heads, virtual * local), BF16),
            pltpu.VMEM((virtual, heads * heads, hs), F32),
            pltpu.VMEM((virtual, seq, seq), F32),
            pltpu.VMEM((virtual, tokens, width), BF16),
            pltpu.VMEM((peers, heads * heads, virtual * local), BF16),
            pltpu.VMEM((virtual, heads * heads, hs), F32),
            dma((ROUNDS, virtual, apart, PIECES, PIECES)),
            dma((ROUNDS, virtual, apart, PIECES, PIECES)),
            dma((ROUNDS, virtual, peers, PIECES, PIECES)),
            dma((ROUNDS, virtual, peers, PIECES, PIECES)),
            dma((ROUNDS, virtual, PIECES)),
            dma((ROUNDS, virtual, PIECES)),
            dma((apart,)),
            dma((apart,)),
            dma((4, virtual)),
            dma((1,)),
            dma((1,)),
            dma((virtual, PIECES)),
        ],
        compiler_params=pltpu.CompilerParams(
            collective_id=0, has_side_effects=True, vmem_limit_bytes=56 * 1024 * 1024
        ),
        cost_estimate=pl.CostEstimate(
            flops=ROUNDS * virtual * seq * local_heads * hs * (6 * hs + 4 * seq),
            bytes_accessed=6 * 1024 * 1024,
            transcendentals=ROUNDS * virtual * seq * local_heads * seq,
        ),
    )(
        stream[:, 0],
        gain[:, 0],
        w_query[:, 0],
        w_key[:, 0],
        w_value[:, 0],
        w_mix[:, 0].transpose(0, 2, 3, 1).reshape(virtual, heads * heads, local),
        active[:, 0],
        random_blocks[:, 0],
    )
    return result[:, None]


def solution(mesh):
    in_specs = (
        P(None, "segment", "fsdp", None),
        P(None, "segment", None),
        P(None, "segment", "fsdp", None, None),
        P(None, "segment", "fsdp", None, None),
        P(None, "segment", "fsdp", None, None),
        P(None, "segment", "fsdp", None, None),
        P(None, "segment"),
        P(None, "segment", None, None),
    )
    out_specs = P(None, "segment", "fsdp", None)
    body = functools.partial(shards, mesh.shape["segment"], mesh.shape["fsdp"])
    return jax.shard_map(body, mesh=mesh, in_specs=in_specs, out_specs=out_specs, check_vma=False)
```

```python
import functools

import jax
import jax.numpy as jnp
from jax import lax
from jax.experimental import pallas as pl
from jax.experimental.pallas import tpu as pltpu
from jax.sharding import PartitionSpec as P

BLK = 64
ROUNDS = 2
EPS = 1e-05
LANES = 128
PIECES = 2
GROUPS = 4
MESH = pl.DeviceIdType.MESH
F32 = jnp.float32
BF16 = jnp.bfloat16


def kernel(
    segments, peers, stream_hbm, gain_in, wq_hbm, wk_hbm, wv_hbm, wm, live, ids, out,
    stream, gain, wq, wk, wv,
    st_in, xn, gath, att_out, att_in, st_out, wm_all, wm_t, counts,
    x_send, x_recv, a_send, a_recv, s_send, s_recv, m_send, m_recv, load_sem,
):
    virtual, tokens, width = stream.shape
    local_heads, hs = wq.shape[1], wq.shape[2]
    half = tokens // PIECES
    part = local_heads // GROUPS
    local = wm.shape[2]
    heads = width // hs
    seq = tokens * peers
    blocks = seq // BLK
    randoms = ids.shape[2]
    s = lax.axis_index("segment")
    f = lax.axis_index("fsdp")
    ahead = lax.rem(s + 1, segments)
    behind = lax.rem(s + segments - 1, segments)

    barrier = pltpu.get_barrier_semaphore()
    for d in range(1, peers):
        pl.semaphore_signal(barrier, inc=1, device_id=(s, lax.rem(f + d, peers)), device_id_type=MESH)
    for other in (ahead, behind):
        pl.semaphore_signal(barrier, inc=1, device_id=(other, f), device_id_type=MESH)

    def load(n, v):
        source, target = ((stream_hbm, stream), (wq_hbm, wq), (wk_hbm, wk), (wv_hbm, wv))[n]
        return pltpu.make_async_copy(source.at[v], target.at[v], load_sem.at[n, v])

    for n in range(4):
        for v in range(virtual):
            load(n, v).start()

    def to_peer(d):
        return lax.rem(f + d, peers)

    def from_peer(d):
        return lax.rem(f + peers - d, peers)

    def x_copy(r, v, d, pc, hh, landing=False):
        slot = from_peer(d) if landing else f
        rows, lanes = pl.ds(pc * half, half), pl.ds(hh * part * hs, part * hs)
        return pltpu.make_async_remote_copy(
            src_ref=xn.at[r, v, to_peer(d), rows, lanes], dst_ref=gath.at[r, v, slot, rows, lanes],
            send_sem=x_send.at[r, v, d - 1, pc, hh], recv_sem=x_recv.at[r, v, d - 1, pc, hh],
            device_id=(s, to_peer(d)), device_id_type=MESH)

    def a_copy(r, v, d, pc, hh, landing=False):
        slot = from_peer(d) if landing else f
        rows, lanes = pl.ds(pc * half, half), pl.ds(hh * part * hs, part * hs)
        return pltpu.make_async_remote_copy(
            src_ref=att_out.at[r, v, to_peer(d), rows, lanes], dst_ref=att_in.at[r, v, slot, rows, lanes],
            send_sem=a_send.at[r, v, d - 1, pc, hh], recv_sem=a_recv.at[r, v, d - 1, pc, hh],
            device_id=(s, to_peer(d)), device_id_type=MESH)

    def m_copy(d, landing=False):
        slot = from_peer(d) if landing else f
        return pltpu.make_async_remote_copy(
            src_ref=wm_all.at[f], dst_ref=wm_all.at[slot],
            send_sem=m_send.at[d - 1], recv_sem=m_recv.at[d - 1],
            device_id=(s, to_peer(d)), device_id_type=MESH)

    def s_copy(r, v, pc, side, landing=False):
        at = v if landing else lax.rem(v + jnp.where(s == segments - 1, 1, 0), virtual)
        target = out if r == ROUNDS - 1 else st_in.at[r]
        rows, lanes = pl.ds(pc * half, half), pl.ds(side * (width // 2), width // 2)
        return pltpu.make_async_remote_copy(
            src_ref=st_out.at[r, v, rows, lanes], dst_ref=target.at[at, rows, lanes],
            send_sem=s_send.at[r, v, pc, side], recv_sem=s_recv.at[r, at, pc, side],
            device_id=(ahead, f), device_id_type=MESH)

    def state_of(r):
        return stream if r == 0 else st_in.at[r - 1]

    def order(r):
        if r == 0:
            return list(range(virtual))
        return [lax.rem(o + jnp.where(s < r, 1, 0), virtual) for o in range(virtual)]

    def norm(r, v, pc):
        state = state_of(r)

        def rows_body(i, carry):
            rows = pl.ds(pl.multiple_of(pc * half + i * 16, 16), 16)
            total = jnp.zeros((16, LANES), F32)
            for c in range(width // LANES):
                wide = state[v, rows, c * LANES:(c + 1) * LANES].astype(F32)
                total = total + wide * wide
            scale = lax.rsqrt(jnp.sum(total, axis=1, keepdims=True) / width + EPS)
            for c in range(heads):
                wide = state[v, rows, c * hs:(c + 1) * hs].astype(F32)
                g = gain[v, :, c * hs:(c + 1) * hs]
                j, at = c // local_heads, (c % local_heads) * hs
                xn[r, v, j, rows, at:at + hs] = (wide * scale * g).astype(BF16)
            return carry

        lax.fori_loop(0, half // 16, rows_body, 0)

    def count_blocks():
        lane_block = lax.broadcasted_iota(jnp.int32, (BLK, seq), 1) // BLK
        for v in range(virtual):
            for i in range(blocks):
                window = [(i - 1) % blocks, i, (i + 1) % blocks, 0]
                total = jnp.zeros((BLK, seq), F32)
                for b in window:
                    total = total + jnp.where(lane_block == b, 1.0, 0.0)
                for k in range(randoms):
                    total = total + jnp.where(lane_block == ids[v, i, k], 1.0, 0.0)
                counts[v, i * BLK:(i + 1) * BLK, :] = total

    def attention(r, v, hh):
        step = 4 if part % 4 == 0 else 1

        ones = jnp.ones((seq, hs), BF16)

        def body(i, carry):
            mine = [hh * part + i * step + u for u in range(step)]
            lanes = [pl.ds(pl.multiple_of(h * hs, hs), hs) for h in mine]
            x = [gath[r, v, :, :, at].reshape(seq, hs) for at in lanes]
            qk = [
                jnp.dot(x[u], jnp.concatenate([wq[v, h], wk[v, h]], axis=1), preferred_element_type=F32)
                for u, h in enumerate(mine)
            ]
            q = [(a[:, :hs] * hs ** (-0.5)).astype(BF16) for a in qk]
            k = [a[:, hs:].astype(BF16) for a in qk]
            scores = [
                lax.dot_general(a, b, (((1,), (1,)), ((), ())), preferred_element_type=F32)
                for a, b in zip(q, k)
            ]
            val = [
                jnp.dot(x[u], wv[v, h], preferred_element_type=F32).astype(BF16)
                for u, h in enumerate(mine)
            ]
            count = counts[v]
            if blocks > 3:
                scores = [jnp.where(count > 0.0, a, -3e38) for a in scores]
            top = [jnp.max(a, axis=1, keepdims=True) for a in scores]
            powers = [(jnp.exp(a - m) * count).astype(BF16) for a, m in zip(scores, top)]
            sums = [
                jnp.dot(p, jnp.concatenate([a, ones], axis=1), preferred_element_type=F32)
                for p, a in zip(powers, val)
            ]
            att = [(a[:, :hs] * (1.0 / a[:, hs:])).astype(BF16) for a in sums]
            for at, a in zip(lanes, att):
                att_out[r, v, :, :, at] = a.reshape(peers, tokens, hs)
            return carry

        lax.fori_loop(0, part // step, body, 0)

    def pack_mix():
        def body(i, carry):
            rows = pl.ds(pl.multiple_of(i * LANES, LANES), LANES)
            both = [wm[v, rows, :].astype(F32) for v in range(virtual)]
            wm_all[f, rows, :] = jnp.concatenate(both, axis=1).astype(BF16)
            return carry

        lax.fori_loop(0, heads * heads // LANES, body, 0)

    def spread_mix():
        def body(i, carry):
            rows = pl.ds(pl.multiple_of(i * LANES, LANES), LANES)
            each = [wm_all[j, rows, :].astype(F32) for j in range(peers)]
            for v in range(virtual):
                wm_t[v, rows, :] = jnp.concatenate(
                    [e[:, v * local:(v + 1) * local] for e in each], axis=1)
            return carry

        lax.fori_loop(0, heads * heads // LANES, body, 0)

    def mix(r, v, pc, side):
        state = state_of(r)
        on = jnp.full((half, hs), live[v].astype(F32))

        rows = pl.ds(pc * half, half)

        def body(group, carry):
            sums = [jnp.zeros((half, hs), F32) for _ in range(8)]
            for h in range(heads):
                j, at = h // local_heads, (h % local_heads) * hs
                a = att_in[r, v, j, rows, at:at + hs].astype(F32)
                w = wm_t[v, pl.ds(pl.multiple_of(h * heads + group * 8, 8), 8), :]
                for g in range(8):
                    sums[g] = sums[g] + a * w[g:g + 1]
            for g in range(8):
                lanes = pl.ds(pl.multiple_of((group * 8 + g) * hs, hs), hs)
                wide = state[v, rows, lanes].astype(F32)
                updated = wide + sums[g].astype(BF16).astype(F32)
                st_out[r, v, rows, lanes] = jnp.where(on > 0.0, updated, wide).astype(BF16)
            return carry

        lax.fori_loop(side * (heads // 16), (side + 1) * (heads // 16), body, 0)

    others = range(1, peers)
    pieces = range(PIECES)
    groups = range(GROUPS)
    sides = range(2)

    def send_x(r, v, pc, hh):
        for d in others:
            x_copy(r, v, d, pc, hh).start()

    def send_a(r, v, hh):
        for pc in pieces:
            for d in others:
                a_copy(r, v, d, pc, hh).start()

    def wait_x(r, v, hh):
        for d in others:
            for pc in pieces:
                x_copy(r, v, d, pc, hh, landing=True).wait_recv()

    def wait_a(r, v, pc):
        for d in others:
            for hh in groups:
                a_copy(r, v, d, pc, hh, landing=True).wait_recv()

    for r in range(ROUNDS):
        todo = order(r)
        for o, v in enumerate(todo):
            if r == 0:
                load(0, v).wait()
                gain[v] = gain_in[v:v + 1, :].astype(F32)
            for pc in pieces:
                if r > 0:
                    for side in sides:
                        s_copy(r - 1, v, pc, side, landing=True).wait_recv()
                norm(r, v, pc)
                if r > 0 and o == 0:
                    for hh in groups:
                        send_x(r, v, pc, hh)
            if r == 0 and o == 0:
                pl.semaphore_wait(barrier, peers + 1)
                for hh in groups:
                    for pc in pieces:
                        send_x(r, v, pc, hh)
            gath[r, v, f] = xn[r, v, f]
        if r == 0:
            pack_mix()
            count_blocks()
        for o, v in enumerate(todo):
            if r == 0:
                for n in range(1, 4):
                    load(n, v).wait()
            for hh in groups:
                wait_x(r, v, hh)
                if o + 1 < virtual:
                    for pc in pieces:
                        send_x(r, todo[o + 1], pc, hh)
                if r == 0 and o == 0 and hh == GROUPS - 1:
                    for d in others:
                        m_copy(d).start()
                attention(r, v, hh)
                send_a(r, v, hh)
            att_in[r, v, f] = att_out[r, v, f]
        if r == 0:
            for d in others:
                m_copy(d, landing=True).wait_recv()
            spread_mix()
        for v in todo:
            for pc in pieces:
                wait_a(r, v, pc)
                for side in sides:
                    mix(r, v, pc, side)
                    s_copy(r, v, pc, side).start()

    for v in range(virtual):
        for pc in pieces:
            for side in sides:
                s_copy(ROUNDS - 1, v, pc, side, landing=True).wait_recv()
    for r in range(ROUNDS):
        for v in range(virtual):
            for pc in pieces:
                for d in others:
                    for hh in groups:
                        x_copy(r, v, d, pc, hh).wait_send()
                        a_copy(r, v, d, pc, hh).wait_send()
                for side in sides:
                    s_copy(r, v, pc, side).wait_send()
    for d in others:
        m_copy(d).wait_send()


def copy_kernel(source, target, sem):
    virtual, tokens, _ = source.shape
    count = sem.shape[1]
    step = tokens // count

    def piece(v, i):
        rows = pl.ds(i * step, step)
        return pltpu.make_async_copy(source.at[v, rows], target.at[v, rows], sem.at[v, i])

    for v in range(virtual):
        for i in range(count):
            piece(v, i).start()
    for v in range(virtual):
        for i in range(count):
            piece(v, i).wait()


def shards(segments, peers, stream, gain, w_query, w_key, w_value, w_mix, active, random_blocks):
    virtual, _, tokens, width = stream.shape
    local_heads, hs = w_query.shape[2], w_query.shape[3]
    heads = width // hs
    local = w_mix.shape[2]
    seq = tokens * peers
    group = local_heads * hs
    vmem = pl.BlockSpec(memory_space=pltpu.VMEM)
    hbm = pl.BlockSpec(memory_space=pl.ANY)
    smem = pl.BlockSpec(memory_space=pltpu.SMEM)
    dma = pltpu.SemaphoreType.DMA
    apart = max(peers - 1, 1)
    result = pl.pallas_call(
        functools.partial(kernel, segments, peers),
        out_shape=jax.ShapeDtypeStruct((virtual, tokens, width), BF16),
        in_specs=[hbm, vmem, hbm, hbm, hbm, vmem, smem, smem],
        out_specs=pl.BlockSpec(memory_space=pl.ANY),
        scratch_shapes=[
            pltpu.VMEM((virtual, tokens, width), BF16),
            pltpu.VMEM((virtual, 1, width), F32),
            pltpu.VMEM((virtual, local_heads, hs, hs), BF16),
            pltpu.VMEM((virtual, local_heads, hs, hs), BF16),
            pltpu.VMEM((virtual, local_heads, hs, hs), BF16),
            pltpu.VMEM((max(ROUNDS - 1, 1), virtual, tokens, width), BF16),
            pltpu.VMEM((ROUNDS, virtual, peers, tokens, group), BF16),
            pltpu.VMEM((ROUNDS, virtual, peers, tokens, group), BF16),
            pltpu.VMEM((ROUNDS, virtual, peers, tokens, group), BF16),
            pltpu.VMEM((ROUNDS, virtual, peers, tokens, group), BF16),
            pltpu.VMEM((ROUNDS, virtual, tokens, width), BF16),
            pltpu.VMEM((peers, heads * heads, virtual * local), BF16),
            pltpu.VMEM((virtual, heads * heads, hs), F32),
            pltpu.VMEM((virtual, seq, seq), F32),
            dma((ROUNDS, virtual, apart, PIECES, GROUPS)),
            dma((ROUNDS, virtual, apart, PIECES, GROUPS)),
            dma((ROUNDS, virtual, apart, PIECES, GROUPS)),
            dma((ROUNDS, virtual, apart, PIECES, GROUPS)),
            dma((ROUNDS, virtual, PIECES, 2)),
            dma((ROUNDS, virtual, PIECES, 2)),
            dma((apart,)),
            dma((apart,)),
            dma((4, virtual)),
        ],
        compiler_params=pltpu.CompilerParams(
            collective_id=0, has_side_effects=True, vmem_limit_bytes=56 * 1024 * 1024
        ),
        cost_estimate=pl.CostEstimate(
            flops=ROUNDS * virtual * seq * local_heads * hs * (6 * hs + 4 * seq),
            bytes_accessed=6 * 1024 * 1024,
            transcendentals=ROUNDS * virtual * seq * local_heads * seq,
        ),
    )(
        stream[:, 0],
        gain[:, 0],
        w_query[:, 0],
        w_key[:, 0],
        w_value[:, 0],
        w_mix[:, 0].transpose(0, 2, 3, 1).reshape(virtual, heads * heads, local),
        active[:, 0],
        random_blocks[:, 0],
    )
    written = pl.pallas_call(
        copy_kernel,
        out_shape=jax.ShapeDtypeStruct(result.shape, BF16),
        in_specs=[hbm],
        out_specs=hbm,
        scratch_shapes=[dma((virtual, 4))],
        compiler_params=pltpu.CompilerParams(vmem_limit_bytes=60 * 1024 * 1024),
        cost_estimate=pl.CostEstimate(flops=0, bytes_accessed=4 * virtual * tokens * width, transcendentals=0),
    )(result)
    return written[:, None]


def solution(mesh):
    in_specs = (
        P(None, "segment", "fsdp", None),
        P(None, "segment", None),
        P(None, "segment", "fsdp", None, None),
        P(None, "segment", "fsdp", None, None),
        P(None, "segment", "fsdp", None, None),
        P(None, "segment", "fsdp", None, None),
        P(None, "segment"),
        P(None, "segment", None, None),
    )
    out_specs = P(None, "segment", "fsdp", None)
    body = functools.partial(shards, mesh.shape["segment"], mesh.shape["fsdp"])
    return jax.shard_map(body, mesh=mesh, in_specs=in_specs, out_specs=out_specs, check_vma=False)
```

```python
import functools

import jax
import jax.numpy as jnp
from jax import lax
from jax.experimental import pallas as pl
from jax.experimental.pallas import tpu as pltpu
from jax.sharding import PartitionSpec as P

BLK = 64
ROUNDS = 2
EPS = 1e-05
LANES = 128
PIECES = 2
MESH = pl.DeviceIdType.MESH
F32 = jnp.float32
BF16 = jnp.bfloat16


def kernel(
    segments, peers, stream_hbm, gain_in, wq_hbm, wk_hbm, wv_hbm, wm, live, ids, out,
    stream, gain, wq, wk, wv,
    st_in, xn, gath, att_out, att_in, st_out, wm_all, wm_t, counts,
    x_send, x_recv, a_send, a_recv, s_send, s_recv, m_send, m_recv, load_sem,
):
    virtual, tokens, width = stream.shape
    local_heads, hs = wq.shape[1], wq.shape[2]
    half = tokens // PIECES
    part = local_heads // PIECES
    local = wm.shape[2]
    heads = width // hs
    seq = tokens * peers
    blocks = seq // BLK
    randoms = ids.shape[2]
    s = lax.axis_index("segment")
    f = lax.axis_index("fsdp")
    ahead = lax.rem(s + 1, segments)
    behind = lax.rem(s + segments - 1, segments)

    barrier = pltpu.get_barrier_semaphore()
    for d in range(1, peers):
        pl.semaphore_signal(barrier, inc=1, device_id=(s, lax.rem(f + d, peers)), device_id_type=MESH)
    for other in (ahead, behind):
        pl.semaphore_signal(barrier, inc=1, device_id=(other, f), device_id_type=MESH)

    def load(n, v):
        source, target = ((stream_hbm, stream), (wq_hbm, wq), (wk_hbm, wk), (wv_hbm, wv))[n]
        return pltpu.make_async_copy(source.at[v], target.at[v], load_sem.at[n, v])

    for n in range(4):
        for v in range(virtual):
            load(n, v).start()

    def to_peer(d):
        return lax.rem(f + d, peers)

    def from_peer(d):
        return lax.rem(f + peers - d, peers)

    def x_copy(r, v, d, pc, hh, landing=False):
        slot = from_peer(d) if landing else f
        rows, lanes = pl.ds(pc * half, half), pl.ds(hh * part * hs, part * hs)
        return pltpu.make_async_remote_copy(
            src_ref=xn.at[r, v, to_peer(d), rows, lanes], dst_ref=gath.at[r, v, slot, rows, lanes],
            send_sem=x_send.at[r, v, d - 1, pc, hh], recv_sem=x_recv.at[r, v, d - 1, pc, hh],
            device_id=(s, to_peer(d)), device_id_type=MESH)

    def a_copy(r, v, d, pc, hh, landing=False):
        slot = from_peer(d) if landing else f
        rows, lanes = pl.ds(pc * half, half), pl.ds(hh * part * hs, part * hs)
        return pltpu.make_async_remote_copy(
            src_ref=att_out.at[r, v, to_peer(d), rows, lanes], dst_ref=att_in.at[r, v, slot, rows, lanes],
            send_sem=a_send.at[r, v, d - 1, pc, hh], recv_sem=a_recv.at[r, v, d - 1, pc, hh],
            device_id=(s, to_peer(d)), device_id_type=MESH)

    def m_copy(d, landing=False):
        slot = from_peer(d) if landing else f
        return pltpu.make_async_remote_copy(
            src_ref=wm_all.at[f], dst_ref=wm_all.at[slot],
            send_sem=m_send.at[d - 1], recv_sem=m_recv.at[d - 1],
            device_id=(s, to_peer(d)), device_id_type=MESH)

    def s_copy(r, v, pc, landing=False):
        at = v if landing else lax.rem(v + jnp.where(s == segments - 1, 1, 0), virtual)
        target = out if r == ROUNDS - 1 else st_in.at[r]
        rows = pl.ds(pc * half, half)
        return pltpu.make_async_remote_copy(
            src_ref=st_out.at[r, v, rows], dst_ref=target.at[at, rows],
            send_sem=s_send.at[r, v, pc], recv_sem=s_recv.at[r, at, pc],
            device_id=(ahead, f), device_id_type=MESH)

    def state_of(r):
        return stream if r == 0 else st_in.at[r - 1]

    def order(r):
        if r == 0:
            return list(range(virtual))
        return [lax.rem(o + jnp.where(s < r, 1, 0), virtual) for o in range(virtual)]

    def norm(r, v, pc):
        state = state_of(r)

        def rows_body(i, carry):
            rows = pl.ds(pl.multiple_of(pc * half + i * 16, 16), 16)
            total = jnp.zeros((16, LANES), F32)
            for c in range(width // LANES):
                wide = state[v, rows, c * LANES:(c + 1) * LANES].astype(F32)
                total = total + wide * wide
            scale = lax.rsqrt(jnp.sum(total, axis=1, keepdims=True) / width + EPS)
            for c in range(heads):
                wide = state[v, rows, c * hs:(c + 1) * hs].astype(F32)
                g = gain[v, :, c * hs:(c + 1) * hs]
                j, at = c // local_heads, (c % local_heads) * hs
                xn[r, v, j, rows, at:at + hs] = (wide * scale * g).astype(BF16)
            return carry

        lax.fori_loop(0, half // 16, rows_body, 0)

    def count_blocks():
        lane_block = lax.broadcasted_iota(jnp.int32, (BLK, seq), 1) // BLK
        for v in range(virtual):
            for i in range(blocks):
                window = [(i - 1) % blocks, i, (i + 1) % blocks, 0]
                total = jnp.zeros((BLK, seq), F32)
                for b in window:
                    total = total + jnp.where(lane_block == b, 1.0, 0.0)
                for k in range(randoms):
                    total = total + jnp.where(lane_block == ids[v, i, k], 1.0, 0.0)
                counts[v, i * BLK:(i + 1) * BLK, :] = total

    def attention(r, v, hh):
        step = 4 if part % 4 == 0 else 1

        ones = jnp.ones((seq, hs), BF16)

        def body(i, carry):
            mine = [hh * part + i * step + u for u in range(step)]
            lanes = [pl.ds(pl.multiple_of(h * hs, hs), hs) for h in mine]
            x = [gath[r, v, :, :, at].reshape(seq, hs) for at in lanes]
            qk = [
                jnp.dot(x[u], jnp.concatenate([wq[v, h], wk[v, h]], axis=1), preferred_element_type=F32)
                for u, h in enumerate(mine)
            ]
            q = [(a[:, :hs] * hs ** (-0.5)).astype(BF16) for a in qk]
            k = [a[:, hs:].astype(BF16) for a in qk]
            scores = [
                lax.dot_general(a, b, (((1,), (1,)), ((), ())), preferred_element_type=F32)
                for a, b in zip(q, k)
            ]
            val = [
                jnp.dot(x[u], wv[v, h], preferred_element_type=F32).astype(BF16)
                for u, h in enumerate(mine)
            ]
            count = counts[v]
            if blocks > 3:
                scores = [jnp.where(count > 0.0, a, -3e38) for a in scores]
            top = [jnp.max(a, axis=1, keepdims=True) for a in scores]
            powers = [(jnp.exp(a - m) * count).astype(BF16) for a, m in zip(scores, top)]
            sums = [
                jnp.dot(p, jnp.concatenate([a, ones], axis=1), preferred_element_type=F32)
                for p, a in zip(powers, val)
            ]
            att = [(a[:, :hs] * (1.0 / a[:, hs:])).astype(BF16) for a in sums]
            for at, a in zip(lanes, att):
                att_out[r, v, :, :, at] = a.reshape(peers, tokens, hs)
            return carry

        lax.fori_loop(0, part // step, body, 0)

    def pack_mix():
        def body(i, carry):
            rows = pl.ds(pl.multiple_of(i * LANES, LANES), LANES)
            both = [wm[v, rows, :].astype(F32) for v in range(virtual)]
            wm_all[f, rows, :] = jnp.concatenate(both, axis=1).astype(BF16)
            return carry

        lax.fori_loop(0, heads * heads // LANES, body, 0)

    def spread_mix():
        def body(i, carry):
            rows = pl.ds(pl.multiple_of(i * LANES, LANES), LANES)
            each = [wm_all[j, rows, :].astype(F32) for j in range(peers)]
            for v in range(virtual):
                wm_t[v, rows, :] = jnp.concatenate(
                    [e[:, v * local:(v + 1) * local] for e in each], axis=1)
            return carry

        lax.fori_loop(0, heads * heads // LANES, body, 0)

    def mix(r, v, pc):
        state = state_of(r)
        on = jnp.full((half, hs), live[v].astype(F32))

        rows = pl.ds(pc * half, half)

        def body(group, carry):
            sums = [jnp.zeros((half, hs), F32) for _ in range(8)]
            for h in range(heads):
                j, at = h // local_heads, (h % local_heads) * hs
                a = att_in[r, v, j, rows, at:at + hs].astype(F32)
                w = wm_t[v, pl.ds(pl.multiple_of(h * heads + group * 8, 8), 8), :]
                for g in range(8):
                    sums[g] = sums[g] + a * w[g:g + 1]
            for g in range(8):
                lanes = pl.ds(pl.multiple_of((group * 8 + g) * hs, hs), hs)
                wide = state[v, rows, lanes].astype(F32)
                updated = wide + sums[g].astype(BF16).astype(F32)
                st_out[r, v, rows, lanes] = jnp.where(on > 0.0, updated, wide).astype(BF16)
            return carry

        lax.fori_loop(0, heads // 8, body, 0)

    others = range(1, peers)
    pieces = range(PIECES)
    def send_x(r, v, pc):
        for hh in pieces:
            for d in others:
                x_copy(r, v, d, pc, hh).start()

    def send_a(r, v, hh):
        for pc in pieces:
            for d in others:
                a_copy(r, v, d, pc, hh).start()

    def wait_x(r, v, hh):
        for d in others:
            for pc in pieces:
                x_copy(r, v, d, pc, hh, landing=True).wait_recv()

    def wait_a(r, v, pc):
        for d in others:
            for hh in pieces:
                a_copy(r, v, d, pc, hh, landing=True).wait_recv()

    for r in range(ROUNDS):
        todo = order(r)
        for o, v in enumerate(todo):
            if r == 0:
                load(0, v).wait()
                gain[v] = gain_in[v:v + 1, :].astype(F32)
            for pc in pieces:
                if r > 0:
                    s_copy(r - 1, v, pc, landing=True).wait_recv()
                norm(r, v, pc)
                if r == 0 and o == 0 and pc == 0:
                    pl.semaphore_wait(barrier, peers + 1)
                if o == 0:
                    send_x(r, v, pc)
            gath[r, v, f] = xn[r, v, f]
        if r == 0:
            pack_mix()
            count_blocks()
        for o, v in enumerate(todo):
            if r == 0:
                for n in range(1, 4):
                    load(n, v).wait()
            for hh in pieces:
                wait_x(r, v, hh)
                if hh == 0:
                    if o + 1 < virtual:
                        for pc in pieces:
                            send_x(r, todo[o + 1], pc)
                    if r == 0 and o == 0:
                        for d in others:
                            m_copy(d).start()
                attention(r, v, hh)
                if o == 0:
                    send_a(r, v, hh)
            att_in[r, v, f] = att_out[r, v, f]
        if r == 0:
            for d in others:
                m_copy(d, landing=True).wait_recv()
            spread_mix()
        for o, v in enumerate(todo):
            for pc in pieces:
                wait_a(r, v, pc)
                if pc == 0 and o + 1 < virtual:
                    for hh in pieces:
                        send_a(r, todo[o + 1], hh)
                mix(r, v, pc)
                s_copy(r, v, pc).start()

    for v in range(virtual):
        for pc in pieces:
            s_copy(ROUNDS - 1, v, pc, landing=True).wait_recv()
    for r in range(ROUNDS):
        for v in range(virtual):
            for pc in pieces:
                for d in others:
                    for hh in pieces:
                        x_copy(r, v, d, pc, hh).wait_send()
                        a_copy(r, v, d, pc, hh).wait_send()
                s_copy(r, v, pc).wait_send()
    for d in others:
        m_copy(d).wait_send()


def copy_kernel(source, target):
    target[...] = source[...]


def shards(segments, peers, stream, gain, w_query, w_key, w_value, w_mix, active, random_blocks):
    virtual, _, tokens, width = stream.shape
    local_heads, hs = w_query.shape[2], w_query.shape[3]
    heads = width // hs
    local = w_mix.shape[2]
    seq = tokens * peers
    group = local_heads * hs
    vmem = pl.BlockSpec(memory_space=pltpu.VMEM)
    hbm = pl.BlockSpec(memory_space=pl.ANY)
    smem = pl.BlockSpec(memory_space=pltpu.SMEM)
    dma = pltpu.SemaphoreType.DMA
    apart = max(peers - 1, 1)
    result = pl.pallas_call(
        functools.partial(kernel, segments, peers),
        out_shape=jax.ShapeDtypeStruct((virtual, tokens, width), BF16),
        in_specs=[hbm, vmem, hbm, hbm, hbm, vmem, smem, smem],
        out_specs=pl.BlockSpec(memory_space=pl.ANY),
        scratch_shapes=[
            pltpu.VMEM((virtual, tokens, width), BF16),
            pltpu.VMEM((virtual, 1, width), F32),
            pltpu.VMEM((virtual, local_heads, hs, hs), BF16),
            pltpu.VMEM((virtual, local_heads, hs, hs), BF16),
            pltpu.VMEM((virtual, local_heads, hs, hs), BF16),
            pltpu.VMEM((max(ROUNDS - 1, 1), virtual, tokens, width), BF16),
            pltpu.VMEM((ROUNDS, virtual, peers, tokens, group), BF16),
            pltpu.VMEM((ROUNDS, virtual, peers, tokens, group), BF16),
            pltpu.VMEM((ROUNDS, virtual, peers, tokens, group), BF16),
            pltpu.VMEM((ROUNDS, virtual, peers, tokens, group), BF16),
            pltpu.VMEM((ROUNDS, virtual, tokens, width), BF16),
            pltpu.VMEM((peers, heads * heads, virtual * local), BF16),
            pltpu.VMEM((virtual, heads * heads, hs), F32),
            pltpu.VMEM((virtual, seq, seq), F32),
            dma((ROUNDS, virtual, apart, PIECES, PIECES)),
            dma((ROUNDS, virtual, apart, PIECES, PIECES)),
            dma((ROUNDS, virtual, apart, PIECES, PIECES)),
            dma((ROUNDS, virtual, apart, PIECES, PIECES)),
            dma((ROUNDS, virtual, PIECES)),
            dma((ROUNDS, virtual, PIECES)),
            dma((apart,)),
            dma((apart,)),
            dma((4, virtual)),
        ],
        compiler_params=pltpu.CompilerParams(
            collective_id=0, has_side_effects=True, vmem_limit_bytes=56 * 1024 * 1024
        ),
        cost_estimate=pl.CostEstimate(
            flops=ROUNDS * virtual * seq * local_heads * hs * (6 * hs + 4 * seq),
            bytes_accessed=6 * 1024 * 1024,
            transcendentals=ROUNDS * virtual * seq * local_heads * seq,
        ),
    )(
        stream[:, 0],
        gain[:, 0],
        w_query[:, 0],
        w_key[:, 0],
        w_value[:, 0],
        w_mix[:, 0].transpose(0, 2, 3, 1).reshape(virtual, heads * heads, local),
        active[:, 0],
        random_blocks[:, 0],
    )
    block = pl.BlockSpec((1, tokens // PIECES, width), lambda v, i: (v, i, 0))
    written = pl.pallas_call(
        copy_kernel,
        grid=(virtual, PIECES),
        out_shape=jax.ShapeDtypeStruct(result.shape, BF16),
        in_specs=[block],
        out_specs=block,
        compiler_params=pltpu.CompilerParams(vmem_limit_bytes=60 * 1024 * 1024),
    )(result)
    return written[:, None]


def solution(mesh):
    in_specs = (
        P(None, "segment", "fsdp", None),
        P(None, "segment", None),
        P(None, "segment", "fsdp", None, None),
        P(None, "segment", "fsdp", None, None),
        P(None, "segment", "fsdp", None, None),
        P(None, "segment", "fsdp", None, None),
        P(None, "segment"),
        P(None, "segment", None, None),
    )
    out_specs = P(None, "segment", "fsdp", None)
    body = functools.partial(shards, mesh.shape["segment"], mesh.shape["fsdp"])
    return jax.shard_map(body, mesh=mesh, in_specs=in_specs, out_specs=out_specs, check_vma=False)
```
